512 devices in a mesh: grp: 2 (over core), ctx: 32 (over x_lo, z), kvh: 8 (over y, x_hi).
Axes of the slice: x: 4 (x_hi: 2, x_lo: 2; x = x_hi * 2 + x_lo), y: 4, z: 16, core: 2. Of those that a mesh axis runs over, the one named last changes fastest.
Arguments:
- slab_query: bfloat16 [2, 256, 8, 12, 128], P('grp', 'ctx', 'kvh'), may hold values from -32 to 32
- kv_cache: bfloat16 [2, 2, 65536, 8, 128], P('grp', None, 'ctx', 'kvh'), may hold values from -32 to 32
- kept_list: int32 [2, 8, 384], P(None, 'kvh'), may hold values from 0 to 511, as said below
- decode_place: int32 [2, 8, 384], P(None, 'kvh'), may hold values from 0 to 31, as said below
- step_query: bfloat16 [2, 2, 8, 12, 128], P('grp', None, 'kvh'), may hold values from -32 to 32
- step_cache: bfloat16 [2, 2, 2, 8, 128], P('grp', None, None, 'kvh'), may hold values from -16 to 16
Outputs:
- slab_out: bfloat16 [2, 256, 8, 12, 128], P('grp', 'ctx', 'kvh')
- heavy_score: float32 [2, 8, 65536], P('grp', 'kvh', 'ctx')
- paged_cache: bfloat16 [2, 8, 2, 384, 128, 128], P('grp', 'kvh', None, 'ctx')
- step_out: bfloat16 [2, 2, 8, 12, 128], P('grp', None, 'kvh')
The draws below stay inside these ranges and needn't reach their ends.
Inputs may be any that keep to these rules, and one draw needn't show every extreme that they name: `kept_list`: for each sequence and KV head, 384 different block numbers in increasing order; the last 16 blocks of the sequence are always among them. `decode_place`: entry i is the index along ctx of the decode device of block kept_list[., ., i]; in each aligned run of 32 entries (r * 32 to r * 32 + 31) every decode device appears exactly once; the kept blocks of one head that lie on one prefill device go to different decode devices.
All inputs are finite; a program needn't handle non-finite values.
Results may differ from the reference program's by a relative error of at most 0.0075.
Values may be sent and summed in bfloat16 or wider, within the bound.
No kernel may reach another device: no remote copies, remote signals or barrier semaphores. Data moves between devices by JAX's collectives and lax.ppermute only.
A program may use at most 64 MiB of HBM per device.

```python
import math
import jax
import jax.numpy as jnp
from jax import lax

HD = 128
GQ = 12
BLK = 128
SLAB = 256
STEPS = 2
KVH = 8
SEQS = 2
LEN = 65536
BPD = 16
NBLK = 512
KEEP = 384
SLOTS = 12
N_CTX = 32


def draw_kv_cache(key, part):
    key = jax.random.fold_in(key, 1)
    subkeys = jax.random.split(key, 2)
    full_shape = (SEQS, 2, LEN, KVH, HD)
    position = jnp.arange(LEN, dtype=jnp.float32) / LEN
    raw_draw = jax.random.truncated_normal(subkeys[0], -4.0, 4.0, full_shape, jnp.float32)
    spread = jnp.exp(jax.random.uniform(subkeys[1], (SEQS, LEN, KVH, 1), jnp.float32, math.log(0.3), math.log(3.0)))
    ramp_scale = 0.8 + 0.6 * position
    key_part = raw_draw[:, 0] * spread * ramp_scale[None, :, None, None]
    value_part = raw_draw[:, 1]
    return jnp.stack([key_part, value_part], axis=1).astype(jnp.bfloat16)


def draw_slab_query(key, part):
    key = jax.random.fold_in(key, 2)
    subkeys = jax.random.split(key, 2)
    full_shape = (SEQS, SLAB, KVH, GQ, HD)
    raw_draw = jax.random.truncated_normal(subkeys[0], -4.0, 4.0, full_shape, jnp.float32)
    spread = jnp.exp(jax.random.uniform(subkeys[1], (SEQS, SLAB, KVH, GQ, 1), jnp.float32, math.log(0.3), math.log(3.0)))
    queries = raw_draw * spread
    return queries.astype(jnp.bfloat16)


def draw_step_query(key, part):
    key = jax.random.fold_in(key, 3)
    subkeys = jax.random.split(key, 2)
    full_shape = (SEQS, STEPS, KVH, GQ, HD)
    raw_draw = jax.random.truncated_normal(subkeys[0], -4.0, 4.0, full_shape, jnp.float32)
    spread = jnp.exp(jax.random.uniform(subkeys[1], (SEQS, STEPS, KVH, GQ, 1), jnp.float32, math.log(0.3), math.log(3.0)))
    queries = raw_draw * spread
    return queries.astype(jnp.bfloat16)


def kept_routes(key):
    key = jax.random.fold_in(key, 11)
    subkeys = jax.random.split(key, 3)
    block_index = jnp.arange(NBLK, dtype=jnp.int32)
    keep_noise = jax.random.randint(subkeys[0], (SEQS, KVH, NBLK), 0, 4096)
    favour = block_index * 4096 // NBLK + jnp.where(block_index >= NBLK - BPD, 1048576, 0)
    keep_score = (keep_noise + favour) * NBLK + block_index
    chosen = lax.top_k(keep_score, KEEP)[1]
    kept_blocks = jnp.sort(chosen, axis=-1).astype(jnp.int32)
    owner_dev = (kept_blocks // BPD).reshape(SEQS, KVH, SLOTS, N_CTX)
    last_owner = owner_dev[..., -1]
    before = jnp.concatenate([jnp.full((SEQS, KVH, 1), -1, jnp.int32), last_owner[..., :-1]], axis=-1)
    dest_noise = jax.random.randint(subkeys[1], (SLOTS, SEQS, KVH, N_CTX), 0, 1048576)
    spot_noise = jax.random.randint(subkeys[2], (SLOTS, SEQS, KVH, N_CTX), 0, 1048576)
    lane_ids = jnp.arange(N_CTX, dtype=jnp.int32)

    def one_round(used_mask, round_inputs):
        owners, previous, round_last, dest_rand, spot_rand = round_inputs
        lead_mask = (owners == previous[..., None]).astype(jnp.int32)
        dest_key = (dest_rand + used_mask * 2097152) * N_CTX + lane_ids
        spot_key = (spot_rand - lead_mask * 2097152) * N_CTX + lane_ids
        dest_order = jnp.argsort(dest_key, axis=-1)
        spot_rank = jnp.argsort(jnp.argsort(spot_key, axis=-1), axis=-1)
        dest_ids = jnp.take_along_axis(dest_order, spot_rank, axis=-1).astype(jnp.int32)
        tail_mask = owners == round_last[..., None]
        hits = (dest_ids[..., :, None] == lane_ids).astype(jnp.int32)
        used_mask = jnp.sum(jnp.where(tail_mask[..., :, None], hits, 0), axis=-2).astype(jnp.int32)
        return (used_mask, dest_ids)
    round_inputs = (jnp.moveaxis(owner_dev, 2, 0), jnp.moveaxis(before, 2, 0), jnp.moveaxis(last_owner, 2, 0), dest_noise, spot_noise)
    _, dest_ids = lax.scan(one_round, jnp.zeros((SEQS, KVH, N_CTX), jnp.int32), round_inputs)
    placed = jnp.moveaxis(dest_ids, 0, 2).reshape(SEQS, KVH, KEEP).astype(jnp.int32)
    return (kept_blocks, placed)


def draw_kept_list(key, part):
    return kept_routes(key)[0]


def draw_decode_place(key, part):
    return kept_routes(key)[1]


def levels(own_key, dims, pieces, least, largest):
    factor_of = 1.0
    for axis_at, shards_of in pieces:
        heights = jax.random.uniform(jax.random.fold_in(jax.random.fold_in(own_key, 6), axis_at), (shards_of,), jnp.float32, least / len(pieces), largest / len(pieces))
        factor_of = factor_of * jnp.repeat(jnp.exp(heights), dims[axis_at] // shards_of).reshape((-1,) + (1,) * (len(dims) - 1 - axis_at))
    return factor_of


def gaussian(rng, shape, width, most, cuts=(), held_as=jnp.bfloat16):
    values = jax.random.normal(rng, shape, jnp.float32) * width
    if len(cuts) > 0:
        values = levels(rng, shape, cuts, -0.22, 0.18) * values
    return jnp.clip(values, min=-most, max=most).astype(held_as)


def setup_inputs(seed: int = 0) -> dict:
    seeds = jax.random.split(jax.random.key(seed), 7)
    slab_query = draw_slab_query(jax.random.fold_in(seeds[6], 71), 0)
    kv_cache = draw_kv_cache(jax.random.fold_in(seeds[6], 71), 0)
    kept_list = draw_kept_list(jax.random.fold_in(seeds[6], 71), 0)
    decode_place = draw_decode_place(jax.random.fold_in(seeds[6], 71), 0)
    step_query = draw_step_query(jax.random.fold_in(seeds[6], 71), 0)
    step_cache = gaussian(seeds[5], (SEQS, 2, STEPS, KVH, HD), 4.0, 16.0, ((0, 2), (3, 8)))
    return {"slab_query": slab_query, "kv_cache": kv_cache, "kept_list": kept_list, "decode_place": decode_place, "step_query": step_query, "step_cache": step_cache}


def prefill_head(row_set, key_all, value_all, score_scale):
    count_rows = row_set.shape[0]
    key_block = math.gcd(LEN, 8192)
    count_blocks = LEN // key_block
    row_pos = LEN - SLAB + jnp.arange(count_rows, dtype=jnp.int32) // GQ
    key_pos = jnp.arange(LEN, dtype=jnp.int32).reshape(count_blocks, key_block)
    key_sets = key_all.reshape(count_blocks, key_block, HD)
    value_sets = value_all.reshape(count_blocks, key_block, HD)

    def scores_of(key_set, pos_set):
        scores = jnp.dot(row_set, key_set.T, preferred_element_type=jnp.float32) * score_scale
        return (scores, pos_set[None, :] <= row_pos[:, None])

    def peak_step(row_peak, inputs):
        scores, seen_mask = scores_of(inputs[0], inputs[1])
        return (jnp.maximum(row_peak, lax.optimization_barrier(jnp.max(jnp.where(seen_mask, scores, -jnp.inf), axis=1))), None)
    row_peak, _ = lax.scan(peak_step, jnp.full((count_rows,), -jnp.inf, jnp.float32), (key_sets, key_pos))

    def total_step(row_total, inputs):
        scores, seen_mask = scores_of(inputs[0], inputs[1])
        return (row_total + lax.optimization_barrier(jnp.sum(jnp.where(seen_mask, jnp.exp(scores - row_peak[:, None]), 0.0), axis=1)), None)
    row_total, _ = lax.scan(total_step, jnp.zeros((count_rows,), jnp.float32), (key_sets, key_pos))

    def final_step(accumulated, inputs):
        scores, seen_mask = scores_of(inputs[0], inputs[2])
        weight = jnp.where(seen_mask, jnp.exp(scores - row_peak[:, None]) / row_total[:, None], 0.0)
        accumulated = accumulated + jnp.dot(weight.astype(jnp.bfloat16), inputs[1], preferred_element_type=jnp.float32)
        return (accumulated, lax.optimization_barrier(jnp.sum(weight, axis=0)))
    accumulated, column = lax.scan(final_step, jnp.zeros((count_rows, HD), jnp.float32), (key_sets, value_sets, key_pos))
    return (accumulated.astype(jnp.bfloat16), column.reshape(LEN) * (LEN / (GQ * SLAB)))

def decode_head(cache_pair, chosen, placed, queries, new_keys, new_values, score_scale):
    blocks = cache_pair.reshape(2, NBLK, BLK, HD)
    slot_index = placed * SLOTS + jnp.arange(KEEP, dtype=jnp.int32) // N_CTX
    slot_order = jnp.argsort(slot_index)
    paged_blocks = jnp.take(blocks, jnp.take(chosen, slot_order), axis=1)
    key_rows = paged_blocks[0].reshape(KEEP * BLK, HD)
    value_rows = paged_blocks[1].reshape(KEEP * BLK, HD)
    query_rows = queries.reshape(STEPS * GQ, HD)
    cache_scores = jnp.dot(query_rows, key_rows.T, preferred_element_type=jnp.float32) * score_scale
    new_scores = jnp.dot(query_rows, new_keys.T, preferred_element_type=jnp.float32) * score_scale
    row_step = jnp.arange(STEPS * GQ, dtype=jnp.int32) // GQ
    visible = jnp.arange(STEPS, dtype=jnp.int32)[None, :] <= row_step[:, None]
    row_peak = jnp.maximum(lax.optimization_barrier(jnp.max(cache_scores, axis=1)), lax.optimization_barrier(jnp.max(jnp.where(visible, new_scores, -jnp.inf), axis=1)))
    cache_weight = jnp.exp(cache_scores - row_peak[:, None])
    new_weight = jnp.where(visible, jnp.exp(new_scores - row_peak[:, None]), 0.0)
    row_total = lax.optimization_barrier(jnp.sum(cache_weight, axis=1)) + lax.optimization_barrier(jnp.sum(new_weight, axis=1))
    accumulated = jnp.dot(cache_weight, value_rows.astype(jnp.float32), precision=lax.Precision.HIGHEST)
    accumulated = accumulated + jnp.dot(new_weight, new_values.astype(jnp.float32), precision=lax.Precision.HIGHEST)
    result = (accumulated / row_total[:, None]).astype(jnp.bfloat16)
    return (paged_blocks, result.reshape(STEPS, GQ, HD))

def reference(slab_query, kv_cache, kept_list, decode_place, step_query, step_cache):
    score_scale = 1.0 / math.sqrt(HD)
    row_sets = jnp.transpose(slab_query, (0, 2, 1, 3, 4)).reshape(SEQS * KVH, SLAB * GQ, HD)
    key_sets = jnp.transpose(kv_cache[:, 0], (0, 2, 1, 3)).reshape(SEQS * KVH, LEN, HD)
    value_sets = jnp.transpose(kv_cache[:, 1], (0, 2, 1, 3)).reshape(SEQS * KVH, LEN, HD)
    head_outs, columns = lax.map(lambda inputs: prefill_head(inputs[0], inputs[1], inputs[2], score_scale), (row_sets, key_sets, value_sets))
    slab_out = jnp.transpose(head_outs.reshape(SEQS, KVH, SLAB, GQ, HD), (0, 2, 1, 3, 4))
    heavy_score = columns.reshape(SEQS, KVH, LEN)
    paged_list = []
    step_list = []
    for decode_group in range(SEQS):
        other_seq = SEQS - 1 - decode_group
        cache_pairs = jnp.moveaxis(kv_cache[other_seq], 2, 0)
        paged_blocks, results = jax.vmap(decode_head, in_axes=(0, 0, 0, 0, 0, 0, None))(cache_pairs, kept_list[other_seq], decode_place[other_seq], jnp.transpose(step_query[decode_group], (1, 0, 2, 3)), jnp.transpose(step_cache[decode_group, 0], (1, 0, 2)), jnp.transpose(step_cache[decode_group, 1], (1, 0, 2)), score_scale)
        paged_list.append(paged_blocks)
        step_list.append(jnp.transpose(results, (1, 0, 2, 3)))
    return (slab_out, heavy_score, jnp.stack(paged_list, axis=0), jnp.stack(step_list, axis=0))
```

```python
import math

import jax
import jax.numpy as jnp
from jax import lax
from jax.experimental import pallas as pl
from jax.experimental.pallas import tpu as pltpu
from jax.sharding import Mesh
from jax.sharding import PartitionSpec as P

BLK = 128
HD = 128
NZ = 16
NCTX = 32
ROWS = 96
HALF = NZ * ROWS
CTXL = 2048
SLAB = 256
RB = 384
NRB = HALF // RB
PER = RB // ROWS
SLOTS = 12
STEPR = 24
NEG = -1e30
C2 = math.log2(math.e) / math.sqrt(HD)
BF = jnp.bfloat16
F32 = jnp.float32

STAT = 3 * NZ
DEC = 32
XROWS = HALF + STAT + DEC
ZROWS = ROWS + STAT + DEC


def params(mib=40):
    return pltpu.CompilerParams(vmem_limit_bytes=mib * 1024 * 1024)


def parts_of(x):
    hi = x.astype(BF).astype(F32)
    mid = (x - hi).astype(BF).astype(F32)
    return hi, mid, x - hi - mid


def column(row):
    return jnp.broadcast_to(row, (128, 128)).T


def scores_t(k, q):
    return lax.dot_general(k, q, (((1,), (1,)), ((), ())), preferred_element_type=F32)


def mask_tail(info_ref, i, s_ref):
    @pl.when(info_ref[0] == NCTX - 1)
    def _():
        tail = s_ref[CTXL - SLAB :, :]
        key = lax.broadcasted_iota(jnp.int32, tail.shape, 0)
        row = lax.broadcasted_iota(jnp.int32, tail.shape, 1) + i * RB
        token = info_ref[1] * (SLAB // 2) + (row // ROWS) * 8 + row % 8
        s_ref[CTXL - SLAB :, :] = jnp.where(key <= token, tail, NEG)


def fill_vt(v, vt_ref):
    vt_ref[0:HD, :] = v.astype(F32).T.astype(BF)
    vt_ref[HD:, :] = jnp.ones((16, CTXL), BF)


def flash_kernel(info_ref, q_ref, k_ref, v_ref, d_ref, x_ref, vt_ref, s_ref, lse_ref):
    i = pl.program_id(0)

    @pl.when(i == 0)
    def _():
        fill_vt(v_ref[0], vt_ref)
        lse_ref[...] = jnp.zeros_like(lse_ref)

    s_ref[...] = scores_t(k_ref[0], q_ref[...])
    mask_tail(info_ref, i, s_ref)
    top = jnp.max(s_ref[...], axis=0, keepdims=True)
    p = jnp.exp2((s_ref[...] - top) * C2).astype(BF)
    acc = jnp.dot(vt_ref[...], p, preferred_element_type=F32)
    mass = acc[HD : HD + 1]
    x_ref[pl.ds(pl.multiple_of(i * RB, RB), RB), :] = (acc[0:HD] * (1.0 / mass)).T.astype(BF)
    lse = top * C2 + jnp.log2(mass)
    for j in range(PER):
        lse_ref[pl.ds(i * PER + j, 1), 0:ROWS] = lse[:, j * ROWS : (j + 1) * ROWS]

    @pl.when(i == NRB - 1)
    def _():
        for n, part in enumerate(parts_of(lse_ref[...])):
            x_ref[HALF + n * NZ : HALF + (n + 1) * NZ, :] = part.astype(BF)
        x_ref[HALF + STAT :, :] = d_ref[...]


def flash(info, q, kv, dec):
    return pl.pallas_call(
        flash_kernel,
        out_shape=jax.ShapeDtypeStruct((XROWS, HD), BF),
        grid=(NRB,),
        in_specs=[
            pl.BlockSpec(memory_space=pltpu.SMEM),
            pl.BlockSpec((RB, HD), lambda i: (i, 0)),
            pl.BlockSpec((1, CTXL, HD), lambda i: (0, 0, 0)),
            pl.BlockSpec((1, CTXL, HD), lambda i: (1, 0, 0)),
            pl.BlockSpec((DEC, HD), lambda i: (0, 0)),
        ],
        out_specs=pl.BlockSpec((XROWS, HD), lambda i: (0, 0)),
        scratch_shapes=[
            pltpu.VMEM((HD + 16, CTXL), BF),
            pltpu.VMEM((CTXL, RB), F32),
            pltpu.VMEM((NZ, HD), F32),
        ],
        compiler_params=params(),
        cost_estimate=pl.CostEstimate(
            flops=4 * HALF * CTXL * HD, bytes_accessed=2 * CTXL * HD * 2, transcendentals=HALF * CTXL
        ),
        name="slab_partial",
    )(info, q, kv, kv, dec)


def decode_kernel(flag_ref, q_ref, k_ref, v_ref, d_ref, vt_ref, s_ref, t_ref):
    fill_vt(v_ref[0], vt_ref)
    for b in range(CTXL // BLK):
        s = scores_t(k_ref[0, b * BLK : (b + 1) * BLK, :], q_ref[...])
        kept = jnp.broadcast_to(flag_ref[b], s.shape) > 0
        s_ref[b * BLK : (b + 1) * BLK, :] = jnp.where(kept, s, NEG)
    top = jnp.max(s_ref[...], axis=0, keepdims=True)
    p = jnp.exp2((s_ref[...] - top) * C2).astype(BF)
    acc = jnp.dot(vt_ref[...], p, preferred_element_type=F32)
    mass = acc[HD : HD + 1]
    out = (acc[0:HD] * (1.0 / mass)).T
    lse = jnp.maximum(top * C2 + jnp.log2(mass), NEG)
    put_decode(t_ref, out[0:STEPR], lse, d_ref)


def put_decode(t_ref, out, lse, d_ref):
    t_ref[...] = jnp.zeros_like(t_ref)
    t_ref[0:STEPR, :] = out
    for n, part in enumerate(parts_of(lse)):
        t_ref[STEPR + n : STEPR + n + 1, :] = part
    d_ref[...] = t_ref[...].astype(BF)


def decode_partial(flags, q, kv):
    return pl.pallas_call(
        decode_kernel,
        out_shape=jax.ShapeDtypeStruct((DEC, HD), BF),
        grid=(1,),
        in_specs=[
            pl.BlockSpec(memory_space=pltpu.SMEM),
            pl.BlockSpec((HD, HD), lambda i: (0, 0)),
            pl.BlockSpec((1, CTXL, HD), lambda i: (0, 0, 0)),
            pl.BlockSpec((1, CTXL, HD), lambda i: (1, 0, 0)),
        ],
        out_specs=pl.BlockSpec((DEC, HD), lambda i: (0, 0)),
        scratch_shapes=[
            pltpu.VMEM((HD + 16, CTXL), BF),
            pltpu.VMEM((CTXL, HD), F32),
            pltpu.VMEM((DEC, HD), F32),
        ],
        compiler_params=params(),
        name="decode_partial",
    )(flags, q, kv, kv)


def stats_of(x):
    return x[0:NZ].astype(F32) + x[NZ : 2 * NZ].astype(F32) + x[2 * NZ : 3 * NZ].astype(F32)


def dec_of(x):
    d = x.astype(F32)
    return d[0:STEPR], d[STEPR : STEPR + 1] + d[STEPR + 1 : STEPR + 2] + d[STEPR + 2 : STEPR + 3]


def merge_weights(lses):
    top = lses[0]
    for x in lses[1:]:
        top = jnp.maximum(top, x)
    es = [jnp.exp2(x - top) for x in lses]
    den = es[0]
    for e in es[1:]:
        den = den + e
    inv = 1.0 / den
    return [e * inv for e in es], top + jnp.log2(den)


def pair_kernel(a_ref, b_ref, z_ref, t_ref):
    la = stats_of(a_ref[HALF : HALF + STAT, :])
    lb = stats_of(b_ref[HALF : HALF + STAT, :])
    (wa, wb), lse = merge_weights([la, lb])
    da, sa = dec_of(a_ref[HALF + STAT :, :])
    db, sb = dec_of(b_ref[HALF + STAT :, :])
    (ua, ub), sd = merge_weights([sa, sb])
    put_decode(t_ref.at[0:DEC], da * column(ua)[0:STEPR] + db * column(ub)[0:STEPR], sd, z_ref.at[0, ROWS + STAT :, :])
    hi, mid, lo = parts_of(lse)
    stat = jnp.concatenate([hi, mid, lo], axis=0).astype(BF)
    dec = z_ref[0, ROWS + STAT :, :]
    for n in range(NZ):
        rows = slice(n * ROWS, (n + 1) * ROWS)
        wide_a = column(wa[n : n + 1])[0:ROWS]
        wide_b = column(wb[n : n + 1])[0:ROWS]
        z_ref[n, 0:ROWS, :] = (a_ref[rows, :].astype(F32) * wide_a + b_ref[rows, :].astype(F32) * wide_b).astype(BF)
        z_ref[n, ROWS : ROWS + STAT, :] = stat
        z_ref[n, ROWS + STAT :, :] = dec


def pair_merge(a, b):
    return pl.pallas_call(
        pair_kernel,
        out_shape=jax.ShapeDtypeStruct((NZ, ZROWS, HD), BF),
        scratch_shapes=[pltpu.VMEM((DEC, HD), F32)],
        compiler_params=params(),
        name="pair_merge",
    )(a, b)


def final_kernel(info_ref, r_ref, q_ref, nk_ref, nv_ref, slab_ref, lse_ref, step_ref, w_ref):
    ws, lse = merge_weights([stats_of(r_ref[s, ROWS : ROWS + STAT, :]) for s in range(NZ)])
    lse_ref[...] = lse
    for s in range(NZ):
        w_ref[s] = ws[s]
    z = info_ref[2]
    total = jnp.zeros((ROWS, HD), F32)
    for s in range(NZ):
        wide = column(w_ref[s, pl.ds(z, 1), :])[0:ROWS]
        total = total + r_ref[s, 0:ROWS, :].astype(F32) * wide
    slab_ref[...] = total.astype(BF)
    decs = [dec_of(r_ref[s, ROWS + STAT :, :]) for s in range(NZ)]
    fresh = scores_t(nk_ref[...], q_ref[...]) * C2
    lane = lax.broadcasted_iota(jnp.int32, (1, HD), 1)
    first = fresh[0:1]
    second = jnp.where(lane % 2 == 1, fresh[1:2], NEG)
    us, _ = merge_weights([d[1] for d in decs] + [first, second])
    nv = nv_ref[...].astype(F32)
    out = column(us[NZ])[0:STEPR] * nv[0:1] + column(us[NZ + 1])[0:STEPR] * nv[1:2]
    for s in range(NZ):
        out = out + decs[s][0] * column(us[s])[0:STEPR]
    step_ref[...] = out.astype(BF)


def final_merge(info, r, q, nk, nv):
    return pl.pallas_call(
        final_kernel,
        out_shape=(
            jax.ShapeDtypeStruct((ROWS, HD), BF),
            jax.ShapeDtypeStruct((NZ, HD), F32),
            jax.ShapeDtypeStruct((STEPR, HD), BF),
        ),
        in_specs=[pl.BlockSpec(memory_space=pltpu.SMEM)] + [pl.BlockSpec(memory_space=pltpu.VMEM)] * 4,
        out_specs=[pl.BlockSpec(memory_space=pltpu.VMEM)] * 3,
        scratch_shapes=[pltpu.VMEM((NZ, NZ, HD), F32)],
        compiler_params=params(),
        name="final_merge",
    )(info, r, q, nk, nv)


def heavy_kernel(info_ref, q_ref, k_ref, lse_ref, prev_ref, h_ref, s_ref, acc_ref):
    i = pl.program_id(0)

    @pl.when(i == 0)
    def _():
        acc_ref[...] = jnp.zeros_like(acc_ref)

    s_ref[...] = scores_t(k_ref[0], q_ref[...])
    mask_tail(info_ref, i, s_ref)
    w = jnp.exp2(s_ref[...] * C2 - lse_ref[0])
    acc_ref[...] += w[:, 0:128] + w[:, 128:256] + w[:, 256:384]

    @pl.when(i == NRB - 1)
    def _():
        ones = jnp.ones((8, 128), F32)
        sums = lax.dot_general(
            ones, acc_ref[...], (((1,), (1,)), ((), ())), precision=lax.Precision.HIGHEST, preferred_element_type=F32
        )
        h_ref[...] = sums[0:1] * (NCTX * CTXL / (12 * SLAB)) + prev_ref[...]


def heavy(info, q, kv, lse, prev):
    return pl.pallas_call(
        heavy_kernel,
        out_shape=jax.ShapeDtypeStruct((1, CTXL), F32),
        grid=(NRB,),
        in_specs=[
            pl.BlockSpec(memory_space=pltpu.SMEM),
            pl.BlockSpec((RB, HD), lambda i: (i, 0)),
            pl.BlockSpec((1, CTXL, HD), lambda i: (0, 0, 0)),
            pl.BlockSpec((1, 1, RB), lambda i: (i, 0, 0)),
            pl.BlockSpec((1, CTXL), lambda i: (0, 0)),
        ],
        out_specs=pl.BlockSpec((1, CTXL), lambda i: (0, 0)),
        scratch_shapes=[pltpu.VMEM((CTXL, RB), F32), pltpu.VMEM((CTXL, HD), F32)],
        compiler_params=params(),
        cost_estimate=pl.CostEstimate(
            flops=2 * HALF * CTXL * HD, bytes_accessed=CTXL * HD * 2, transcendentals=HALF * CTXL
        ),
        name="heavy_columns",
    )(info, q, kv, lse, prev)


def pack_kernel(pick_ref, kv_ref, dep_ref, out_ref, sems):
    copies = [
        pltpu.make_async_copy(kv_ref.at[:, pick_ref[d]], out_ref.at[d], sems.at[d]) for d in range(NCTX)
    ]
    for copy in copies:
        copy.start()
    for copy in copies:
        copy.wait()


def pack(pick, blocks, after):
    return pl.pallas_call(
        pack_kernel,
        out_shape=jax.ShapeDtypeStruct((NCTX, 2, BLK, HD), BF),
        in_specs=[
            pl.BlockSpec(memory_space=pltpu.SMEM),
            pl.BlockSpec(memory_space=pl.ANY),
            pl.BlockSpec(memory_space=pl.ANY),
        ],
        out_specs=pl.BlockSpec(memory_space=pl.ANY),
        scratch_shapes=[pltpu.SemaphoreType.DMA((NCTX,))],
        name="pack_blocks",
    )(pick, blocks, after)


def select_kernel(src_ref, in_ref, out_ref, sems):
    copies = [
        pltpu.make_async_copy(in_ref.at[src_ref[r]], out_ref.at[:, r], sems.at[r]) for r in range(SLOTS)
    ]
    for copy in copies:
        copy.start()
    for copy in copies:
        copy.wait()


def select(source, arrived):
    return pl.pallas_call(
        select_kernel,
        out_shape=jax.ShapeDtypeStruct((2, SLOTS, BLK, HD), BF),
        in_specs=[pl.BlockSpec(memory_space=pltpu.SMEM), pl.BlockSpec(memory_space=pl.ANY)],
        out_specs=pl.BlockSpec(memory_space=pl.ANY),
        scratch_shapes=[pltpu.SemaphoreType.DMA((SLOTS,))],
        name="select_slots",
    )(source, arrived)


SWAP = [(0, 1), (1, 0)]


def local(slab_query, kv_cache, kept_list, decode_place, step_query, step_cache):
    grp = lax.axis_index("grp")
    xl = lax.axis_index("xl")
    z = lax.axis_index("z")
    ctx = xl * NZ + z
    per_dev = CTXL // BLK

    own_list = lax.dynamic_index_in_dim(kept_list, grp, 0, keepdims=False)[0]
    own_place = lax.dynamic_index_in_dim(decode_place, grp, 0, keepdims=False)[0]
    lanes = jnp.arange(NCTX, dtype=jnp.int32)
    offset = own_list - ctx * per_dev
    mine = (offset >= 0) & (offset < per_dev)
    hit = mine[None, :] & (own_place[None, :] == lanes[:, None])
    pick = jnp.clip(jnp.sum(jnp.where(hit, offset[None, :], 0), axis=1), 0, per_dev - 1)
    flags = jnp.sum(
        (offset[None, :] == jnp.arange(per_dev, dtype=jnp.int32)[:, None]).astype(jnp.int32), axis=1
    )
    here = (own_place == ctx).reshape(SLOTS, NCTX)
    source = jnp.clip(
        jnp.sum(jnp.where(here, own_list.reshape(SLOTS, NCTX) // per_dev, 0), axis=1), 0, NCTX - 1
    )
    info_own = jnp.stack([ctx, xl, z]).astype(jnp.int32)
    info_other = jnp.stack([ctx, 1 - xl, z]).astype(jnp.int32)

    q = jnp.transpose(slab_query[0, :, 0], (1, 0, 2)).reshape(ROWS, HD)
    kv = kv_cache[0, :, :, 0]
    steps = jnp.transpose(step_query[0, :, 0], (1, 0, 2)).reshape(STEPR, HD)
    steps = jnp.pad(steps, ((0, HD - STEPR), (0, 0)))
    new = jnp.pad(step_cache[0, :, :, 0], ((0, 0), (0, 14), (0, 0)))

    dec = decode_partial(flags, lax.ppermute(steps, "grp", SWAP), kv)
    dec = lax.ppermute(dec, "grp", SWAP)
    q_own = lax.all_gather(q, "z", axis=0, tiled=True)
    outgoing = pack(pick, kv.reshape(2, per_dev, BLK, HD), q_own)
    arrived = lax.all_to_all(outgoing, ("xl", "z"), 0, 0, tiled=True)

    q_other = lax.ppermute(q_own, "xl", SWAP)
    part_own = flash(info_own, q_own, kv, dec)
    part_other = flash(info_other, q_other, kv, dec)
    part_partner = lax.ppermute(part_other, "xl", SWAP)
    merged = pair_merge(part_own, part_partner)
    received = lax.all_to_all(merged, "z", 0, 0, tiled=True)
    slab, lse, step = final_merge(info_own, received, steps, new[0], new[1])
    lse_own = lse[:, 0:ROWS].reshape(NRB, 1, RB)
    lse_other = lax.ppermute(lse_own, "xl", SWAP)
    columns = heavy(info_own, q_own, kv, lse_own, jnp.zeros((1, CTXL), F32))
    columns = heavy(info_other, q_other, kv, lse_other, columns)

    paged = lax.ppermute(select(source, arrived), "grp", SWAP)

    slab_out = jnp.transpose(slab.reshape(12, 8, HD), (1, 0, 2))[None, :, None]
    step_out = jnp.transpose(step.reshape(12, 2, HD), (1, 0, 2))[None, :, None]
    return (slab_out, columns[None], paged[None, None], step_out)


def solution(mesh):
    split = Mesh(mesh.devices.reshape(2, 2, NZ, 8), ("grp", "xl", "z", "kvh"))
    ctx = ("xl", "z")
    return jax.shard_map(
        local,
        mesh=split,
        in_specs=(
            P("grp", ctx, "kvh", None, None),
            P("grp", None, ctx, "kvh", None),
            P(None, "kvh", None),
            P(None, "kvh", None),
            P("grp", None, "kvh", None, None),
            P("grp", None, None, "kvh", None),
        ),
        out_specs=(
            P("grp", ctx, "kvh", None, None),
            P("grp", "kvh", ctx),
            P("grp", "kvh", None, ctx, None, None),
            P("grp", None, "kvh", None, None),
        ),
        check_vma=False,
    )
```

```python
import functools
import math

import jax
import jax.numpy as jnp
from jax import lax
from jax.experimental import pallas as pl
from jax.experimental.pallas import tpu as pltpu
from jax.sharding import Mesh
from jax.sharding import PartitionSpec as P

BLK = 128
HD = 128
NZ = 16
NCTX = 32
ROWS = 96
HALF = NZ * ROWS
CTXL = 2048
SLAB = 256
RB = 384
NRB = HALF // RB
SLOTS = 12
STEPR = 24
NEG = -1e30
C2 = math.log2(math.e) / math.sqrt(HD)
BF = jnp.bfloat16
F32 = jnp.float32

LR = HALF // HD
DECR = 3 * LR
DSTAT = DECR + STEPR
TAIL = 64
XROWS = HALF + TAIL
ZROWS = ROWS + TAIL
DEC = 32


def params(mib=40):
    return pltpu.CompilerParams(vmem_limit_bytes=mib * 1024 * 1024)


def parts_of(x):
    hi = x.astype(BF).astype(F32)
    mid = (x - hi).astype(BF).astype(F32)
    return hi, mid, x - hi - mid


def column(row):
    return jnp.broadcast_to(row, (128, 128)).T


def scores_t(k, q):
    return lax.dot_general(k, q, (((1,), (1,)), ((), ())), preferred_element_type=F32)


def masked_tail(info_ref, half, i, tail):
    key = lax.broadcasted_iota(jnp.int32, tail.shape, 0)
    row = lax.broadcasted_iota(jnp.int32, tail.shape, 1) + i * RB
    token = half * (SLAB // 2) + (row // ROWS) * 8 + row % 8
    seen = (key <= token) | (info_ref[0] < NCTX - 1)
    return jnp.where(seen, tail, NEG)


def fill_vt(v, vt_ref):
    vt_ref[0:HD, :] = v.astype(F32).T.astype(BF)
    vt_ref[HD:, :] = jnp.ones((16, CTXL), BF)


def put_stats(t_ref, lse, dec, dec_lse):
    for n, part in enumerate(parts_of(lse)):
        t_ref[n * LR : (n + 1) * LR, :] = part
    t_ref[DECR:DSTAT, :] = dec
    for n, part in enumerate(parts_of(dec_lse)):
        t_ref[DSTAT + n : DSTAT + n + 1, :] = part
    t_ref[DSTAT + 3 :, :] = jnp.zeros((TAIL - DSTAT - 3, HD), F32)


def get_stats(t):
    t = t.astype(F32)
    lse = t[0:LR] + t[LR : 2 * LR] + t[2 * LR : 3 * LR]
    dec_lse = t[DSTAT : DSTAT + 1] + t[DSTAT + 1 : DSTAT + 2] + t[DSTAT + 2 : DSTAT + 3]
    return lse, t[DECR:DSTAT], dec_lse


def flash_kernel(other, info_ref, q_ref, k_ref, v_ref, d_ref, x_ref, vt_ref, s_ref, lse_ref, t_ref):
    i = pl.program_id(0)

    @pl.when(i == 0)
    def _():
        fill_vt(v_ref[0], vt_ref)

    s_ref[...] = scores_t(k_ref[0], q_ref[...])
    s_ref[CTXL - SLAB :, :] = masked_tail(info_ref, info_ref[1] ^ other, i, s_ref[CTXL - SLAB :, :])
    top = jnp.max(s_ref[...], axis=0, keepdims=True)
    p = jnp.exp2((s_ref[...] - top) * C2).astype(BF)
    acc = jnp.dot(vt_ref[...], p, preferred_element_type=F32)
    mass = acc[HD : HD + 1]
    x_ref[pl.ds(pl.multiple_of(i * RB, RB), RB), :] = (acc[0:HD] * (1.0 / mass)).T.astype(BF)
    lse = top * C2 + jnp.log2(mass)
    for j in range(RB // HD):
        lse_ref[pl.ds(i * (RB // HD) + j, 1), :] = lse[:, j * HD : (j + 1) * HD]

    @pl.when(i == NRB - 1)
    def _():
        d = d_ref[...]
        put_stats(t_ref, lse_ref[0:LR, :], d[0:STEPR], d[STEPR : STEPR + 1])
        x_ref[HALF:, :] = t_ref[...].astype(BF)


def flash(other, info, q, kv, dec):
    return pl.pallas_call(
        functools.partial(flash_kernel, other),
        out_shape=jax.ShapeDtypeStruct((XROWS, HD), BF),
        grid=(NRB,),
        in_specs=[
            pl.BlockSpec(memory_space=pltpu.SMEM),
            pl.BlockSpec((RB, HD), lambda i: (i, 0)),
            pl.BlockSpec((1, CTXL, HD), lambda i: (0, 0, 0)),
            pl.BlockSpec((1, CTXL, HD), lambda i: (1, 0, 0)),
            pl.BlockSpec((DEC, HD), lambda i: (0, 0)),
        ],
        out_specs=pl.BlockSpec((XROWS, HD), lambda i: (0, 0)),
        scratch_shapes=[
            pltpu.VMEM((HD + 16, CTXL), BF),
            pltpu.VMEM((CTXL, RB), F32),
            pltpu.VMEM((16, HD), F32),
            pltpu.VMEM((TAIL, HD), F32),
        ],
        compiler_params=params(),
        cost_estimate=pl.CostEstimate(
            flops=4 * HALF * CTXL * HD, bytes_accessed=2 * CTXL * HD * 2, transcendentals=HALF * CTXL
        ),
        name="slab_partial",
    )(info, q, kv, kv, dec)


def decode_kernel(flag_ref, q_ref, k_ref, v_ref, d_ref, vt_ref, s_ref):
    fill_vt(v_ref[0], vt_ref)
    for b in range(CTXL // BLK):
        s = scores_t(k_ref[0, b * BLK : (b + 1) * BLK, :], q_ref[...])
        kept = jnp.broadcast_to(flag_ref[b], s.shape) > 0
        s_ref[b * BLK : (b + 1) * BLK, :] = jnp.where(kept, s, NEG)
    top = jnp.max(s_ref[...], axis=0, keepdims=True)
    p = jnp.exp2((s_ref[...] - top) * C2).astype(BF)
    acc = jnp.dot(vt_ref[...], p, preferred_element_type=F32)
    mass = acc[HD : HD + 1]
    out = (acc[0:HD] * (1.0 / mass)).T
    lse = jnp.maximum(top * C2 + jnp.log2(mass), NEG)
    d_ref[...] = jnp.zeros_like(d_ref)
    d_ref[0:STEPR, :] = out[0:STEPR]
    d_ref[STEPR : STEPR + 1, :] = lse


def decode_partial(flags, q, kv):
    return pl.pallas_call(
        decode_kernel,
        out_shape=jax.ShapeDtypeStruct((DEC, HD), F32),
        grid=(1,),
        in_specs=[
            pl.BlockSpec(memory_space=pltpu.SMEM),
            pl.BlockSpec((HD, HD), lambda i: (0, 0)),
            pl.BlockSpec((1, CTXL, HD), lambda i: (0, 0, 0)),
            pl.BlockSpec((1, CTXL, HD), lambda i: (1, 0, 0)),
        ],
        out_specs=pl.BlockSpec((DEC, HD), lambda i: (0, 0)),
        scratch_shapes=[
            pltpu.VMEM((HD + 16, CTXL), BF),
            pltpu.VMEM((CTXL, HD), F32),
        ],
        compiler_params=params(),
        name="decode_partial",
    )(flags, q, kv, kv)


def merge_weights(lses):
    top = lses[0]
    for x in lses[1:]:
        top = jnp.maximum(top, x)
    es = [jnp.exp2(x - top) for x in lses]
    den = es[0]
    for e in es[1:]:
        den = den + e
    inv = 1.0 / den
    return [e * inv for e in es], top + jnp.log2(den)


def pair_kernel(a_ref, b_ref, z_ref, t_ref):
    la, da, sa = get_stats(a_ref[HALF:, :])
    lb, db, sb = get_stats(b_ref[HALF:, :])
    (wa, wb), lse = merge_weights([la, lb])
    (ua, ub), sd = merge_weights([sa, sb])
    put_stats(t_ref, lse, da * column(ua)[0:STEPR] + db * column(ub)[0:STEPR], sd)
    tail = t_ref[...].astype(BF)
    for n in range(NZ):
        z_ref[n, ROWS:, :] = tail
    for g in range(LR):
        rows = slice(g * HD, (g + 1) * HD)
        mixed = a_ref[rows, :].astype(F32) * column(wa[g : g + 1]) + b_ref[rows, :].astype(F32) * column(wb[g : g + 1])
        mixed = mixed.astype(BF)
        for j in range(0, HD, 32):
            n, at = divmod(g * HD + j, ROWS)
            z_ref[n, at : at + 32, :] = mixed[j : j + 32]


def pair_merge(a, b):
    return pl.pallas_call(
        pair_kernel,
        out_shape=jax.ShapeDtypeStruct((NZ, ZROWS, HD), BF),
        scratch_shapes=[pltpu.VMEM((TAIL, HD), F32)],
        compiler_params=params(),
        name="pair_merge",
    )(a, b)


def final_kernel(info_ref, r_ref, q_ref, nk_ref, nv_ref, slab_ref, lse_ref, step_ref, l_ref, w_ref):
    stats = [get_stats(r_ref[s, ROWS:, :]) for s in range(NZ)]
    top = stats[0][0]
    for s in range(1, NZ):
        top = jnp.maximum(top, stats[s][0])
    den = jnp.zeros_like(top)
    for s in range(NZ):
        den = den + jnp.exp2(stats[s][0] - top)
        l_ref[0:LR, s, :] = stats[s][0]
        l_ref[LR, s, :] = jnp.zeros((HD,), F32)
    lse = top + jnp.log2(den)
    lse_ref[...] = lse
    l_ref[0:LR, NZ, :] = lse
    l_ref[LR, NZ, :] = jnp.zeros((HD,), F32)
    first = info_ref[2] * ROWS
    both = jnp.concatenate([l_ref[first // HD], l_ref[first // HD + 1]], axis=1)
    own = pltpu.roll(both, (2 * HD - first % HD) % (2 * HD), 1)[:, 0:HD]
    w_ref[...] = jnp.zeros_like(w_ref)
    w_ref[0:NZ, :] = jnp.exp2(own[0:NZ] - own[NZ : NZ + 1])
    weights = w_ref[...].T
    total = jnp.zeros((ROWS, HD), F32)
    for s in range(NZ):
        total = total + r_ref[s, 0:ROWS, :].astype(F32) * weights[0:ROWS, s : s + 1]
    slab_ref[...] = total.astype(BF)
    fresh = scores_t(nk_ref[...], q_ref[...]) * C2
    lane = lax.broadcasted_iota(jnp.int32, (1, HD), 1)
    first_new = fresh[0:1]
    second_new = jnp.where(lane % 2 == 1, fresh[1:2], NEG)
    us, _ = merge_weights([t[2] for t in stats] + [first_new, second_new])
    for s in range(NZ + 2):
        w_ref[s : s + 1, :] = us[s]
    shares = w_ref[...].T
    nv = nv_ref[...].astype(F32)
    out = shares[0:STEPR, NZ : NZ + 1] * nv[0:1] + shares[0:STEPR, NZ + 1 : NZ + 2] * nv[1:2]
    for s in range(NZ):
        out = out + stats[s][1] * shares[0:STEPR, s : s + 1]
    step_ref[...] = out.astype(BF)


def final_merge(info, r, q, nk, nv):
    return pl.pallas_call(
        final_kernel,
        out_shape=(
            jax.ShapeDtypeStruct((ROWS, HD), BF),
            jax.ShapeDtypeStruct((LR, HD), F32),
            jax.ShapeDtypeStruct((STEPR, HD), BF),
        ),
        in_specs=[pl.BlockSpec(memory_space=pltpu.SMEM)] + [pl.BlockSpec(memory_space=pltpu.VMEM)] * 4,
        out_specs=[pl.BlockSpec(memory_space=pltpu.VMEM)] * 3,
        scratch_shapes=[pltpu.VMEM((LR + 1, 24, HD), F32), pltpu.VMEM((HD, HD), F32)],
        compiler_params=params(),
        name="final_merge",
    )(info, r, q, nk, nv)


def heavy_kernel(other, info_ref, q_ref, k_ref, lse_ref, prev_ref, h_ref, acc_ref):
    i = pl.program_id(0)

    @pl.when(i == 0)
    def _():
        acc_ref[...] = jnp.zeros_like(acc_ref)

    q = q_ref[...]
    per = RB // HD
    lse = jnp.concatenate([lse_ref[pl.ds(i * per + j, 1), :] for j in range(per)], axis=1)
    for c in range(CTXL // SLAB):
        keys = slice(c * SLAB, (c + 1) * SLAB)
        s = scores_t(k_ref[0, keys, :], q)
        if c == CTXL // SLAB - 1:
            s = masked_tail(info_ref, info_ref[1] ^ other, i, s)
        w = jnp.exp2(s * C2 - lse)
        acc_ref[keys, :] += w[:, 0:128] + w[:, 128:256] + w[:, 256:384]

    @pl.when(i == NRB - 1)
    def _():
        ones = jnp.ones((8, 128), F32)
        sums = lax.dot_general(
            ones, acc_ref[...], (((1,), (1,)), ((), ())), precision=lax.Precision.HIGHEST, preferred_element_type=F32
        )
        h_ref[...] = sums[0:1] * (NCTX * CTXL / (12 * SLAB)) + prev_ref[...]


def heavy(other, info, q, kv, lse, prev):
    return pl.pallas_call(
        functools.partial(heavy_kernel, other),
        out_shape=jax.ShapeDtypeStruct((1, CTXL), F32),
        grid=(NRB,),
        in_specs=[
            pl.BlockSpec(memory_space=pltpu.SMEM),
            pl.BlockSpec((RB, HD), lambda i: (i, 0)),
            pl.BlockSpec((1, CTXL, HD), lambda i: (0, 0, 0)),
            pl.BlockSpec((LR, HD), lambda i: (0, 0)),
            pl.BlockSpec((1, CTXL), lambda i: (0, 0)),
        ],
        out_specs=pl.BlockSpec((1, CTXL), lambda i: (0, 0)),
        scratch_shapes=[pltpu.VMEM((CTXL, HD), F32)],
        compiler_params=params(),
        cost_estimate=pl.CostEstimate(
            flops=2 * HALF * CTXL * HD, bytes_accessed=CTXL * HD * 2, transcendentals=HALF * CTXL
        ),
        name="heavy_columns",
    )(info, q, kv, lse, prev)


def pack_kernel(pick_ref, kv_ref, out_ref, sems):
    copies = [
        pltpu.make_async_copy(kv_ref.at[n, pick_ref[d]], out_ref.at[d, n], sems.at[n, d])
        for d in range(NCTX)
        for n in range(2)
    ]
    for copy in copies:
        copy.start()
    for copy in copies:
        copy.wait()


def pack(pick, blocks):
    return pl.pallas_call(
        pack_kernel,
        out_shape=jax.ShapeDtypeStruct((NCTX, 2, BLK, HD), BF),
        in_specs=[pl.BlockSpec(memory_space=pltpu.SMEM), pl.BlockSpec(memory_space=pltpu.VMEM)],
        out_specs=pl.BlockSpec(memory_space=pl.ANY),
        scratch_shapes=[pltpu.SemaphoreType.DMA((2, NCTX))],
        compiler_params=params(),
        name="pack_blocks",
    )(pick, blocks)


def after_kernel(x_ref, after_ref, out_ref):
    del x_ref, after_ref, out_ref


def after(x, other):
    return pl.pallas_call(
        after_kernel,
        out_shape=jax.ShapeDtypeStruct(x.shape, x.dtype),
        in_specs=[pl.BlockSpec(memory_space=pl.ANY)] * 2,
        out_specs=pl.BlockSpec(memory_space=pl.ANY),
        input_output_aliases={0: 0},
        name="after",
    )(x, other)


def select_kernel(src_ref, in_ref, out_ref, sems):
    copies = [
        pltpu.make_async_copy(in_ref.at[src_ref[r], n], out_ref.at[n, r], sems.at[n, r])
        for n in range(2)
        for r in range(SLOTS)
    ]
    for copy in copies:
        copy.start()
    for copy in copies:
        copy.wait()


def select(source, arrived):
    return pl.pallas_call(
        select_kernel,
        out_shape=jax.ShapeDtypeStruct((2, SLOTS, BLK, HD), BF),
        in_specs=[pl.BlockSpec(memory_space=pltpu.SMEM), pl.BlockSpec(memory_space=pl.ANY)],
        out_specs=pl.BlockSpec(memory_space=pltpu.VMEM),
        scratch_shapes=[pltpu.SemaphoreType.DMA((2, SLOTS))],
        compiler_params=params(),
        name="select_slots",
    )(source, arrived)


def spread_kernel(q_ref, out_ref):
    for n in range(NZ):
        out_ref[n] = q_ref[...]


def spread(q):
    return pl.pallas_call(
        spread_kernel,
        out_shape=jax.ShapeDtypeStruct((NZ, ROWS, HD), BF),
        compiler_params=params(),
        name="spread_queries",
    )(q)


SWAP = [(0, 1), (1, 0)]


def local(slab_query, kv_cache, kept_list, decode_place, step_query, step_cache):
    grp = lax.axis_index("grp")
    xl = lax.axis_index("xl")
    z = lax.axis_index("z")
    ctx = xl * NZ + z
    per_dev = CTXL // BLK

    kept = lax.dynamic_index_in_dim(kept_list, 1 - grp, 0, keepdims=False)[0]
    place = lax.dynamic_index_in_dim(decode_place, 1 - grp, 0, keepdims=False)[0]
    lanes = jnp.arange(NCTX, dtype=jnp.int32)
    offset = kept - ctx * per_dev
    mine = (offset >= 0) & (offset < per_dev)
    hit = mine[None, :] & (place[None, :] == lanes[:, None])
    pick = jnp.clip(jnp.sum(jnp.where(hit, offset[None, :], 0), axis=1), 0, per_dev - 1)
    flags = jnp.sum(
        (offset[None, :] == jnp.arange(per_dev, dtype=jnp.int32)[:, None]).astype(jnp.int32), axis=1
    )
    here = (place == ctx).reshape(SLOTS, NCTX)
    source = jnp.clip(
        jnp.sum(jnp.where(here, kept.reshape(SLOTS, NCTX) // per_dev, 0), axis=1), 0, NCTX - 1
    )
    info = jnp.stack([ctx, xl, z]).astype(jnp.int32)

    q = jnp.transpose(slab_query[0, :, 0], (1, 0, 2)).reshape(ROWS, HD)
    kv = kv_cache[0, :, :, 0]
    steps = jnp.transpose(step_query[0, :, 0], (1, 0, 2)).reshape(STEPR, HD)
    steps = jnp.pad(steps, ((0, HD - STEPR), (0, 0)))
    new = jnp.pad(step_cache[0, :, :, 0], ((0, 0), (0, 14), (0, 0)))

    q_own = lax.all_to_all(spread(q), "z", 0, 0, tiled=True).reshape(HALF, HD)
    kv_decode = lax.ppermute(kv, "grp", SWAP)
    blocks = kv_decode.reshape(2, per_dev, BLK, HD)
    dec = decode_partial(flags, steps, kv_decode)

    outgoing = after(pack(pick, blocks), q_own)
    arrived = lax.all_to_all(outgoing, ("xl", "z"), 0, 0, tiled=True)
    q_other = lax.ppermute(q_own, "xl", SWAP)
    part_own = flash(0, info, q_own, kv, dec)
    part_other = flash(1, info, q_other, kv, dec)
    part_partner = lax.ppermute(part_other, "xl", SWAP)
    merged = after(pair_merge(part_own, part_partner), arrived)
    received = lax.all_to_all(merged, "z", 0, 0, tiled=True)

    slab, lse, step = final_merge(info, received, steps, new[0], new[1])
    lse_other = lax.ppermute(lse, "xl", SWAP)
    columns = heavy(0, info, q_own, kv, lse, jnp.zeros((1, CTXL), F32))
    columns = heavy(1, info, q_other, kv, lse_other, columns)

    paged = select(source, arrived)

    slab_out = jnp.transpose(slab.reshape(12, 8, HD), (1, 0, 2))[None, :, None]
    step_out = jnp.transpose(step.reshape(12, 2, HD), (1, 0, 2))[None, :, None]
    return (slab_out, columns[None], paged[None, None], step_out)


def solution(mesh):
    split = Mesh(mesh.devices.reshape(2, 2, NZ, 8), ("grp", "xl", "z", "kvh"))
    ctx = ("xl", "z")
    return jax.shard_map(
        local,
        mesh=split,
        in_specs=(
            P("grp", ctx, "kvh", None, None),
            P("grp", None, ctx, "kvh", None),
            P(None, "kvh", None),
            P(None, "kvh", None),
            P("grp", None, "kvh", None, None),
            P("grp", None, None, "kvh", None),
        ),
        out_specs=(
            P("grp", ctx, "kvh", None, None),
            P("grp", "kvh", ctx),
            P("grp", "kvh", None, ctx, None, None),
            P("grp", None, "kvh", None, None),
        ),
        check_vma=False,
    )
```

```python
import functools
import math

import jax
import jax.numpy as jnp
from jax import lax
from jax.experimental import pallas as pl
from jax.experimental.pallas import tpu as pltpu
from jax.sharding import Mesh
from jax.sharding import PartitionSpec as P

BLK = 128
HD = 128
NZ = 16
NCTX = 32
ROWS = 96
HALF = NZ * ROWS
CTXL = 2048
SLAB = 256
RB = 512
NRB = HALF // RB
SLOTS = 12
STEPR = 24
NEG = -1e30
C2 = math.log2(math.e) / math.sqrt(HD)
BF = jnp.bfloat16
F32 = jnp.float32

LR = HALF // HD
DECR = 3 * LR
DSTAT = DECR + STEPR
TAIL = 64
XROWS = HALF + TAIL
NS = NZ // 2
KEEP = NS * ROWS
MROWS = KEEP + TAIL
ZROWS = ROWS + TAIL
DEC = 32


def params(mib=40):
    return pltpu.CompilerParams(vmem_limit_bytes=mib * 1024 * 1024)


def parts_of(x):
    hi = x.astype(BF).astype(F32)
    mid = (x - hi).astype(BF).astype(F32)
    return hi, mid, x - hi - mid


def column(row):
    return jnp.broadcast_to(row, (128, 128)).T


def scores_t(k, q):
    return lax.dot_general(k, q, (((1,), (1,)), ((), ())), preferred_element_type=F32)


def masked_tail(info_ref, half, i, tail):
    key = lax.broadcasted_iota(jnp.int32, tail.shape, 0)
    row = lax.broadcasted_iota(jnp.int32, tail.shape, 1) + i * RB
    token = half * (SLAB // 2) + (row // ROWS) * 8 + row % 8
    seen = (key <= token) | (info_ref[0] < NCTX - 1)
    return jnp.where(seen, tail, NEG)


def fill_vt(v, vt_ref):
    vt_ref[0:HD, :] = v.astype(F32).T.astype(BF)
    vt_ref[HD:, :] = jnp.ones((16, CTXL), BF)


def put_stats(t_ref, lse, dec, dec_lse):
    for n, part in enumerate(parts_of(lse)):
        t_ref[n * LR : (n + 1) * LR, :] = part
    t_ref[DECR:DSTAT, :] = dec
    for n, part in enumerate(parts_of(dec_lse)):
        t_ref[DSTAT + n : DSTAT + n + 1, :] = part
    t_ref[DSTAT + 3 :, :] = jnp.zeros((TAIL - DSTAT - 3, HD), F32)


def get_stats(t):
    t = t.astype(F32)
    lse = t[0:LR] + t[LR : 2 * LR] + t[2 * LR : 3 * LR]
    dec_lse = t[DSTAT : DSTAT + 1] + t[DSTAT + 1 : DSTAT + 2] + t[DSTAT + 2 : DSTAT + 3]
    return lse, t[DECR:DSTAT], dec_lse


def flash_kernel(other, info_ref, q_ref, k_ref, v_ref, d_ref, x_ref, vt_ref, s_ref, lse_ref, t_ref):
    i = pl.program_id(0)

    @pl.when(i == 0)
    def _():
        fill_vt(v_ref[0], vt_ref)

    s_ref[...] = scores_t(k_ref[0], q_ref[...])
    s_ref[CTXL - SLAB :, :] = masked_tail(info_ref, info_ref[1] ^ other, i, s_ref[CTXL - SLAB :, :])
    top = jnp.max(s_ref[...], axis=0, keepdims=True)
    p = jnp.exp2((s_ref[...] - top) * C2).astype(BF)
    acc = jnp.dot(vt_ref[...], p, preferred_element_type=F32)
    mass = acc[HD : HD + 1]
    x_ref[pl.ds(pl.multiple_of(i * RB, RB), RB), :] = (acc[0:HD] * (1.0 / mass)).T.astype(BF)
    lse = top * C2 + jnp.log2(mass)
    for j in range(RB // HD):
        lse_ref[pl.ds(i * (RB // HD) + j, 1), :] = lse[:, j * HD : (j + 1) * HD]

    @pl.when(i == NRB - 1)
    def _():
        d = d_ref[...]
        put_stats(t_ref, lse_ref[0:LR, :], d[0:STEPR], d[STEPR : STEPR + 1])
        x_ref[HALF:, :] = t_ref[...].astype(BF)


def flash(other, info, q, kv, dec):
    return pl.pallas_call(
        functools.partial(flash_kernel, other),
        out_shape=jax.ShapeDtypeStruct((XROWS, HD), BF),
        grid=(NRB,),
        in_specs=[
            pl.BlockSpec(memory_space=pltpu.SMEM),
            pl.BlockSpec((RB, HD), lambda i: (i, 0)),
            pl.BlockSpec((1, CTXL, HD), lambda i: (0, 0, 0)),
            pl.BlockSpec((1, CTXL, HD), lambda i: (1, 0, 0)),
            pl.BlockSpec((DEC, HD), lambda i: (0, 0)),
        ],
        out_specs=pl.BlockSpec((XROWS, HD), lambda i: (0, 0)),
        scratch_shapes=[
            pltpu.VMEM((HD + 16, CTXL), BF),
            pltpu.VMEM((CTXL, RB), F32),
            pltpu.VMEM((16, HD), F32),
            pltpu.VMEM((TAIL, HD), F32),
        ],
        compiler_params=params(),
        cost_estimate=pl.CostEstimate(
            flops=4 * HALF * CTXL * HD, bytes_accessed=2 * CTXL * HD * 2, transcendentals=HALF * CTXL
        ),
        name="slab_partial",
    )(info, q, kv, kv, dec)


def decode_kernel(flag_ref, q_ref, k_ref, v_ref, d_ref, vt_ref, s_ref):
    fill_vt(v_ref[0], vt_ref)
    for b in range(CTXL // BLK):
        s = scores_t(k_ref[0, b * BLK : (b + 1) * BLK, :], q_ref[...])
        kept = jnp.broadcast_to(flag_ref[b], s.shape) > 0
        s_ref[b * BLK : (b + 1) * BLK, :] = jnp.where(kept, s, NEG)
    top = jnp.max(s_ref[...], axis=0, keepdims=True)
    p = jnp.exp2((s_ref[...] - top) * C2).astype(BF)
    acc = jnp.dot(vt_ref[...], p, preferred_element_type=F32)
    mass = acc[HD : HD + 1]
    out = (acc[0:HD] * (1.0 / mass)).T
    lse = jnp.maximum(top * C2 + jnp.log2(mass), NEG)
    d_ref[...] = jnp.zeros_like(d_ref)
    d_ref[0:STEPR, :] = out[0:STEPR]
    d_ref[STEPR : STEPR + 1, :] = lse


def decode_partial(flags, q, kv):
    return pl.pallas_call(
        decode_kernel,
        out_shape=jax.ShapeDtypeStruct((DEC, HD), F32),
        grid=(1,),
        in_specs=[
            pl.BlockSpec(memory_space=pltpu.SMEM),
            pl.BlockSpec((HD, HD), lambda i: (0, 0)),
            pl.BlockSpec((1, CTXL, HD), lambda i: (0, 0, 0)),
            pl.BlockSpec((1, CTXL, HD), lambda i: (1, 0, 0)),
        ],
        out_specs=pl.BlockSpec((DEC, HD), lambda i: (0, 0)),
        scratch_shapes=[
            pltpu.VMEM((HD + 16, CTXL), BF),
            pltpu.VMEM((CTXL, HD), F32),
        ],
        compiler_params=params(),
        name="decode_partial",
    )(flags, q, kv, kv)


def merge_weights(lses):
    top = lses[0]
    for x in lses[1:]:
        top = jnp.maximum(top, x)
    es = [jnp.exp2(x - top) for x in lses]
    den = es[0]
    for e in es[1:]:
        den = den + e
    inv = 1.0 / den
    return [e * inv for e in es], top + jnp.log2(den)


def merge_stats(a, b, t_ref, w_ref):
    la, da, sa = get_stats(a)
    lb, db, sb = get_stats(b)
    (wa, _), lse = merge_weights([la, lb])
    (ua, ub), sd = merge_weights([sa, sb])
    dec = da * column(ua)[0:STEPR] + db * column(ub)[0:STEPR]
    put_stats(t_ref, lse, dec, sd)
    w_ref[0:LR, 0, :] = wa
    w_ref[LR, 0, :] = jnp.zeros((HD,), F32)
    return lse, dec, sd


def mix(a_ref, b_ref, w_ref, k, owner):
    first = owner * ROWS
    both = jnp.concatenate([w_ref[first // HD], w_ref[first // HD + 1]], axis=1)
    share = column(pltpu.roll(both, (2 * HD - first % HD) % (2 * HD), 1)[0:1, 0:HD])[0:ROWS]
    a = a_ref[k * ROWS : (k + 1) * ROWS, :].astype(F32)
    b = b_ref[k * ROWS : (k + 1) * ROWS, :].astype(F32)
    return b + (a - b) * share


def pair_kernel(info_ref, a_ref, b_ref, keep_ref, give_ref, t_ref, w_ref):
    merge_stats(a_ref[HALF:, :], b_ref[HALF:, :], t_ref, w_ref)
    tail = t_ref[...].astype(BF)
    keep_ref[KEEP:, :] = tail
    give_ref[KEEP:, :] = tail
    odd = info_ref[2] % 2 > 0
    for k in range(NS):
        even_rows = mix(a_ref, b_ref, w_ref, 2 * k, 2 * k).astype(BF)
        odd_rows = mix(a_ref, b_ref, w_ref, 2 * k + 1, 2 * k + 1).astype(BF)
        rows = slice(k * ROWS, (k + 1) * ROWS)
        keep_ref[rows, :] = jnp.where(odd, odd_rows, even_rows)
        give_ref[rows, :] = jnp.where(odd, even_rows, odd_rows)


def pair_merge(info, a, b):
    half = jax.ShapeDtypeStruct((MROWS, HD), BF)
    return pl.pallas_call(
        pair_kernel,
        out_shape=(half, half),
        in_specs=[pl.BlockSpec(memory_space=pltpu.SMEM)] + [pl.BlockSpec(memory_space=pltpu.VMEM)] * 2,
        out_specs=[pl.BlockSpec(memory_space=pltpu.VMEM)] * 2,
        scratch_shapes=[pltpu.VMEM((TAIL, HD), F32), pltpu.VMEM((LR + 1, 8, HD), F32)],
        compiler_params=params(),
        name="pair_merge",
    )(info, a, b)


def next_kernel(info_ref, a_ref, b_ref, after_ref, z_ref, t_ref, w_ref):
    merge_stats(a_ref[KEEP:, :], b_ref[KEEP:, :], t_ref, w_ref)
    tail = t_ref[...].astype(BF)
    for k in range(NS):
        z_ref[k, 0:ROWS, :] = mix(a_ref, b_ref, w_ref, k, 2 * k + info_ref[2] % 2).astype(BF)
        z_ref[k, ROWS:, :] = tail


def next_merge(info, a, b, after):
    return pl.pallas_call(
        next_kernel,
        out_shape=jax.ShapeDtypeStruct((NS, ZROWS, HD), BF),
        in_specs=[pl.BlockSpec(memory_space=pltpu.SMEM)] + [pl.BlockSpec(memory_space=pltpu.VMEM)] * 3,
        out_specs=pl.BlockSpec(memory_space=pltpu.VMEM),
        scratch_shapes=[pltpu.VMEM((TAIL, HD), F32), pltpu.VMEM((LR + 1, 8, HD), F32)],
        compiler_params=params(),
        name="next_merge",
    )(info, a, b, after)


def final_kernel(info_ref, r_ref, q_ref, nk_ref, nv_ref, after_ref, slab_ref, lse_ref, step_ref, l_ref, w_ref):
    stats = [get_stats(r_ref[s, ROWS:, :]) for s in range(NS)]
    top = stats[0][0]
    for s in range(1, NS):
        top = jnp.maximum(top, stats[s][0])
    den = jnp.zeros_like(top)
    for s in range(NS):
        den = den + jnp.exp2(stats[s][0] - top)
        l_ref[0:LR, s, :] = stats[s][0]
        l_ref[LR, s, :] = jnp.zeros((HD,), F32)
    lse = top + jnp.log2(den)
    lse_ref[...] = lse
    l_ref[0:LR, NS, :] = lse
    l_ref[LR, NS, :] = jnp.zeros((HD,), F32)
    first = info_ref[2] * ROWS
    both = jnp.concatenate([l_ref[first // HD], l_ref[first // HD + 1]], axis=1)
    own = pltpu.roll(both, (2 * HD - first % HD) % (2 * HD), 1)[:, 0:HD]
    w_ref[...] = jnp.zeros_like(w_ref)
    w_ref[0:NS, :] = jnp.exp2(own[0:NS] - own[NS : NS + 1])
    weights = w_ref[...].T
    total = jnp.zeros((ROWS, HD), F32)
    for s in range(NS):
        total = total + r_ref[s, 0:ROWS, :].astype(F32) * weights[0:ROWS, s : s + 1]
    slab_ref[...] = total.astype(BF)
    fresh = scores_t(nk_ref[...], q_ref[...]) * C2
    lane = lax.broadcasted_iota(jnp.int32, (1, HD), 1)
    first_new = fresh[0:1]
    second_new = jnp.where(lane % 2 == 1, fresh[1:2], NEG)
    us, _ = merge_weights([t[2] for t in stats] + [first_new, second_new])
    for s in range(NS + 2):
        w_ref[s : s + 1, :] = us[s]
    shares = w_ref[...].T
    nv = nv_ref[...].astype(F32)
    out = shares[0:STEPR, NS : NS + 1] * nv[0:1] + shares[0:STEPR, NS + 1 : NS + 2] * nv[1:2]
    for s in range(NS):
        out = out + stats[s][1] * shares[0:STEPR, s : s + 1]
    step_ref[...] = out.astype(BF)


def final_merge(info, r, q, nk, nv, after):
    return pl.pallas_call(
        final_kernel,
        out_shape=(
            jax.ShapeDtypeStruct((ROWS, HD), BF),
            jax.ShapeDtypeStruct((LR, HD), F32),
            jax.ShapeDtypeStruct((STEPR, HD), BF),
        ),
        in_specs=[pl.BlockSpec(memory_space=pltpu.SMEM)] + [pl.BlockSpec(memory_space=pltpu.VMEM)] * 5,
        out_specs=[pl.BlockSpec(memory_space=pltpu.VMEM)] * 3,
        scratch_shapes=[pltpu.VMEM((LR + 1, 16, HD), F32), pltpu.VMEM((HD, HD), F32)],
        compiler_params=params(),
        name="final_merge",
    )(info, r, q, nk, nv, after)


def heavy_kernel(other, info_ref, q_ref, k_ref, lse_ref, prev_ref, h_ref, acc_ref):
    i = pl.program_id(0)

    @pl.when(i == 0)
    def _():
        acc_ref[...] = jnp.zeros_like(acc_ref)

    q = q_ref[...]
    per = RB // HD
    lse = jnp.concatenate([lse_ref[pl.ds(i * per + j, 1), :] for j in range(per)], axis=1)
    for c in range(CTXL // SLAB):
        keys = slice(c * SLAB, (c + 1) * SLAB)
        s = scores_t(k_ref[0, keys, :], q)
        if c == CTXL // SLAB - 1:
            s = masked_tail(info_ref, info_ref[1] ^ other, i, s)
        w = jnp.exp2(s * C2 - lse)
        acc_ref[keys, :] += (w[:, 0:128] + w[:, 128:256]) + (w[:, 256:384] + w[:, 384:512])

    @pl.when(i == NRB - 1)
    def _():
        for t in range(CTXL // HD):
            at = slice(t * HD, (t + 1) * HD)
            sums = jnp.sum(acc_ref[at, :].T, axis=0, keepdims=True)
            h_ref[:, at] = sums * (NCTX * CTXL / (12 * SLAB)) + prev_ref[:, at]


def heavy(other, info, q, kv, lse, prev):
    return pl.pallas_call(
        functools.partial(heavy_kernel, other),
        out_shape=jax.ShapeDtypeStruct((1, CTXL), F32),
        grid=(NRB,),
        in_specs=[
            pl.BlockSpec(memory_space=pltpu.SMEM),
            pl.BlockSpec((RB, HD), lambda i: (i, 0)),
            pl.BlockSpec((1, CTXL, HD), lambda i: (0, 0, 0)),
            pl.BlockSpec((LR, HD), lambda i: (0, 0)),
            pl.BlockSpec((1, CTXL), lambda i: (0, 0)),
        ],
        out_specs=pl.BlockSpec((1, CTXL), lambda i: (0, 0)),
        scratch_shapes=[pltpu.VMEM((CTXL, HD), F32)],
        compiler_params=params(),
        cost_estimate=pl.CostEstimate(
            flops=2 * HALF * CTXL * HD, bytes_accessed=CTXL * HD * 2, transcendentals=HALF * CTXL
        ),
        name="heavy_columns",
    )(info, q, kv, lse, prev)


def pack_kernel(pick_ref, kv_ref, out_ref, sems):
    copies = [
        pltpu.make_async_copy(kv_ref.at[n, pick_ref[d]], out_ref.at[d, n], sems.at[n, d])
        for d in range(NCTX)
        for n in range(2)
    ]
    for copy in copies:
        copy.start()
    for copy in copies:
        copy.wait()


def pack(pick, blocks):
    return pl.pallas_call(
        pack_kernel,
        out_shape=jax.ShapeDtypeStruct((NCTX, 2, BLK, HD), BF),
        in_specs=[pl.BlockSpec(memory_space=pltpu.SMEM), pl.BlockSpec(memory_space=pltpu.VMEM)],
        out_specs=pl.BlockSpec(memory_space=pl.ANY),
        scratch_shapes=[pltpu.SemaphoreType.DMA((2, NCTX))],
        compiler_params=params(),
        name="pack_blocks",
    )(pick, blocks)


def select_kernel(src_ref, in_ref, out_ref, sems):
    copies = [
        pltpu.make_async_copy(in_ref.at[src_ref[r], n], out_ref.at[n, r], sems.at[n, r])
        for n in range(2)
        for r in range(SLOTS)
    ]
    for copy in copies:
        copy.start()
    for copy in copies:
        copy.wait()


def select(source, arrived):
    return pl.pallas_call(
        select_kernel,
        out_shape=jax.ShapeDtypeStruct((2, SLOTS, BLK, HD), BF),
        in_specs=[pl.BlockSpec(memory_space=pltpu.SMEM), pl.BlockSpec(memory_space=pl.ANY)],
        out_specs=pl.BlockSpec(memory_space=pltpu.VMEM),
        scratch_shapes=[pltpu.SemaphoreType.DMA((2, SLOTS))],
        compiler_params=params(),
        name="select_slots",
    )(source, arrived)


def spread_kernel(q_ref, out_ref):
    for n in range(NZ):
        out_ref[n] = q_ref[...]


def spread(q):
    return pl.pallas_call(
        spread_kernel,
        out_shape=jax.ShapeDtypeStruct((NZ, ROWS, HD), BF),
        compiler_params=params(),
        name="spread_queries",
    )(q)


SWAP = [(0, 1), (1, 0)]


Z = ("zh", "zp")
CTX = ("xl", "zh", "zp")


def local(slab_query, kv_cache, kept_list, decode_place, step_query, step_cache):
    grp = lax.axis_index("grp")
    xl = lax.axis_index("xl")
    z = lax.axis_index("zh") * 2 + lax.axis_index("zp")
    ctx = xl * NZ + z
    per_dev = CTXL // BLK

    kept = lax.dynamic_index_in_dim(kept_list, 1 - grp, 0, keepdims=False)[0]
    place = lax.dynamic_index_in_dim(decode_place, 1 - grp, 0, keepdims=False)[0]
    lanes = jnp.arange(NCTX, dtype=jnp.int32)
    offset = kept - ctx * per_dev
    mine = (offset >= 0) & (offset < per_dev)
    hit = mine[None, :] & (place[None, :] == lanes[:, None])
    pick = jnp.clip(jnp.sum(jnp.where(hit, offset[None, :], 0), axis=1), 0, per_dev - 1)
    flags = jnp.sum(
        (offset[None, :] == jnp.arange(per_dev, dtype=jnp.int32)[:, None]).astype(jnp.int32), axis=1
    )
    here = (place == ctx).reshape(SLOTS, NCTX)
    source = jnp.clip(
        jnp.sum(jnp.where(here, kept.reshape(SLOTS, NCTX) // per_dev, 0), axis=1), 0, NCTX - 1
    )
    info = jnp.stack([ctx, xl, z]).astype(jnp.int32)

    q = jnp.transpose(slab_query[0, :, 0], (1, 0, 2)).reshape(ROWS, HD)
    kv = kv_cache[0, :, :, 0]
    steps = jnp.transpose(step_query[0, :, 0], (1, 0, 2)).reshape(STEPR, HD)
    steps = jnp.pad(steps, ((0, HD - STEPR), (0, 0)))
    new = jnp.pad(step_cache[0, :, :, 0], ((0, 0), (0, 14), (0, 0)))

    q_own = lax.all_to_all(spread(q), Z, 0, 0, tiled=True).reshape(HALF, HD)
    kv_decode = lax.ppermute(kv, "grp", SWAP)
    blocks = kv_decode.reshape(2, per_dev, BLK, HD)
    dec = decode_partial(flags, steps, kv_decode)

    arrived = lax.all_to_all(pack(pick, blocks), CTX, 0, 0, tiled=True)
    q_other = lax.ppermute(q_own, "xl", SWAP)
    part_own = flash(0, info, q_own, kv, dec)
    part_other = flash(1, info, q_other, kv, dec)
    part_partner = lax.ppermute(part_other, "xl", SWAP)
    keep, give = pair_merge(info, part_own, part_partner)
    merged = next_merge(info, keep, lax.ppermute(give, "zp", SWAP), arrived[0, 0, 0:16])
    received = lax.all_to_all(merged, "zh", 0, 0, tiled=True)
    paged = select(source, arrived)
    slab, lse, step = final_merge(info, received, steps, new[0], new[1], paged[0, 0, 0:16])
    lse_other = lax.ppermute(lse, "xl", SWAP)
    columns = heavy(0, info, q_own, kv, lse, jnp.zeros((1, CTXL), F32))
    columns = heavy(1, info, q_other, kv, lse_other, columns)

    slab_out = jnp.transpose(slab.reshape(12, 8, HD), (1, 0, 2))[None, :, None]
    step_out = jnp.transpose(step.reshape(12, 2, HD), (1, 0, 2))[None, :, None]
    return (slab_out, columns[None], paged[None, None], step_out)


def solution(mesh):
    split = Mesh(mesh.devices.reshape(2, 2, NS, 2, 8), ("grp", "xl", "zh", "zp", "kvh"))
    return jax.shard_map(
        local,
        mesh=split,
        in_specs=(
            P("grp", CTX, "kvh", None, None),
            P("grp", None, CTX, "kvh", None),
            P(None, "kvh", None),
            P(None, "kvh", None),
            P("grp", None, "kvh", None, None),
            P("grp", None, None, "kvh", None),
        ),
        out_specs=(
            P("grp", CTX, "kvh", None, None),
            P("grp", "kvh", CTX),
            P("grp", "kvh", None, CTX, None, None),
            P("grp", None, "kvh", None, None),
        ),
        check_vma=False,
    )
```

```python
import functools
import math

import jax
import jax.numpy as jnp
from jax import lax
from jax.experimental import pallas as pl
from jax.experimental.pallas import tpu as pltpu
from jax.sharding import Mesh
from jax.sharding import PartitionSpec as P

BLK = 128
HD = 128
NZ = 16
NCTX = 32
ROWS = 96
HALF = NZ * ROWS
CTXL = 2048
SLAB = 256
RB = 512
NRB = HALF // RB
SLOTS = 12
STEPR = 24
NEG = -1e30
C2 = math.log2(math.e) / math.sqrt(HD)
BF = jnp.bfloat16
F32 = jnp.float32

LR = HALF // HD
NQ = 4
QROWS = NZ // NQ * ROWS
FIRST = 32
DECR = 6 * LR
DSTAT = DECR + STEPR
TAIL = 112
DEC = 32


def params(mib=40):
    return pltpu.CompilerParams(vmem_limit_bytes=mib * 1024 * 1024)


def parts_of(x):
    hi = x.astype(BF).astype(F32)
    mid = (x - hi).astype(BF).astype(F32)
    return hi, mid, x - hi - mid


def column(row):
    return jnp.broadcast_to(row, (128, 128)).T


def scores_t(k, q):
    return lax.dot_general(k, q, (((1,), (1,)), ((), ())), preferred_element_type=F32)


def masked_tail(info_ref, half, i, tail):
    key = lax.broadcasted_iota(jnp.int32, tail.shape, 0)
    row = lax.broadcasted_iota(jnp.int32, tail.shape, 1) + i * RB
    token = half * (SLAB // 2) + (row // ROWS) * 8 + row % 8
    seen = (key <= token) | (info_ref[0] < NCTX - 1)
    return jnp.where(seen, tail, NEG)


def fill_vt(v, vt_ref):
    vt_ref[0:HD, :] = v.astype(F32).T.astype(BF)
    vt_ref[HD:, :] = jnp.ones((16, CTXL), BF)


def put_tail(t_ref, lses, dec, dec_lse):
    for m, lse in enumerate(lses):
        for n, part in enumerate(parts_of(lse)):
            t_ref[(3 * m + n) * LR : (3 * m + n + 1) * LR, :] = part
    t_ref[DECR:DSTAT, :] = dec
    for n, part in enumerate(parts_of(dec_lse)):
        t_ref[DSTAT + n : DSTAT + n + 1, :] = part
    t_ref[DSTAT + 3 :, :] = jnp.zeros((TAIL - DSTAT - 3, HD), F32)


def get_tail(t):
    t = t.astype(F32)
    lses = [sum(t[(3 * m + n) * LR : (3 * m + n + 1) * LR] for n in range(3)) for m in range(2)]
    dec_lse = t[DSTAT : DSTAT + 1] + t[DSTAT + 1 : DSTAT + 2] + t[DSTAT + 2 : DSTAT + 3]
    return lses, t[DECR:DSTAT], dec_lse


def flash_kernel(other, info_ref, q_ref, k_ref, v_ref, after_ref, x_ref, lse_ref, vt_ref, s_ref):
    i = pl.program_id(0)

    @pl.when(i == 0)
    def _():
        fill_vt(v_ref[0], vt_ref)

    s_ref[...] = scores_t(k_ref[0], q_ref[...])
    s_ref[CTXL - SLAB :, :] = masked_tail(info_ref, info_ref[1] ^ other, i, s_ref[CTXL - SLAB :, :])
    top = jnp.max(s_ref[...], axis=0, keepdims=True)
    p = jnp.exp2((s_ref[...] - top) * C2).astype(BF)
    acc = jnp.dot(vt_ref[...], p, preferred_element_type=F32)
    mass = acc[HD : HD + 1]
    x_ref[...] = (acc[0:HD] * (1.0 / mass)).T.astype(BF)
    lse = top * C2 + jnp.log2(mass)
    for j in range(RB // HD):
        lse_ref[pl.ds(i * (RB // HD) + j, 1), :] = lse[:, j * HD : (j + 1) * HD]


def flash(other, info, q, kv, after):
    return pl.pallas_call(
        functools.partial(flash_kernel, other),
        out_shape=(jax.ShapeDtypeStruct((HALF, HD), BF), jax.ShapeDtypeStruct((LR, HD), F32)),
        grid=(NRB,),
        in_specs=[
            pl.BlockSpec(memory_space=pltpu.SMEM),
            pl.BlockSpec((RB, HD), lambda i: (i, 0)),
            pl.BlockSpec((1, CTXL, HD), lambda i: (0, 0, 0)),
            pl.BlockSpec((1, CTXL, HD), lambda i: (1, 0, 0)),
            pl.BlockSpec((8, HD), lambda i: (0, 0)),
        ],
        out_specs=(pl.BlockSpec((RB, HD), lambda i: (i, 0)), pl.BlockSpec((LR, HD), lambda i: (0, 0))),
        scratch_shapes=[pltpu.VMEM((HD + 16, CTXL), BF), pltpu.VMEM((CTXL, RB), F32)],
        compiler_params=params(),
        cost_estimate=pl.CostEstimate(
            flops=20000000000, bytes_accessed=2 * CTXL * HD * 2, transcendentals=HALF * CTXL
        ),
        name="slab_partial",
    )(info, q, kv, kv, after)


def decode_kernel(flag_ref, q_ref, k_ref, v_ref, d_ref, vt_ref, s_ref):
    fill_vt(v_ref[0], vt_ref)
    for b in range(CTXL // BLK):
        s = scores_t(k_ref[0, b * BLK : (b + 1) * BLK, :], q_ref[...])
        kept = jnp.broadcast_to(flag_ref[b], s.shape) > 0
        s_ref[b * BLK : (b + 1) * BLK, :] = jnp.where(kept, s, NEG)
    top = jnp.max(s_ref[...], axis=0, keepdims=True)
    p = jnp.exp2((s_ref[...] - top) * C2).astype(BF)
    acc = jnp.dot(vt_ref[...], p, preferred_element_type=F32)
    mass = acc[HD : HD + 1]
    out = (acc[0:HD] * (1.0 / mass)).T
    lse = jnp.maximum(top * C2 + jnp.log2(mass), NEG)
    d_ref[...] = jnp.zeros_like(d_ref)
    d_ref[0:STEPR, :] = out[0:STEPR]
    d_ref[STEPR : STEPR + 1, :] = lse


def decode_partial(flags, q, kv):
    return pl.pallas_call(
        decode_kernel,
        out_shape=jax.ShapeDtypeStruct((DEC, HD), F32),
        grid=(1,),
        in_specs=[
            pl.BlockSpec(memory_space=pltpu.SMEM),
            pl.BlockSpec((HD, HD), lambda i: (0, 0)),
            pl.BlockSpec((1, CTXL, HD), lambda i: (0, 0, 0)),
            pl.BlockSpec((1, CTXL, HD), lambda i: (1, 0, 0)),
        ],
        out_specs=pl.BlockSpec((DEC, HD), lambda i: (0, 0)),
        scratch_shapes=[
            pltpu.VMEM((HD + 16, CTXL), BF),
            pltpu.VMEM((CTXL, HD), F32),
        ],
        compiler_params=params(),
        name="decode_partial",
    )(flags, q, kv, kv)


def merge_weights(lses):
    top = lses[0]
    for x in lses[1:]:
        top = jnp.maximum(top, x)
    es = [jnp.exp2(x - top) for x in lses]
    den = es[0]
    for e in es[1:]:
        den = den + e
    inv = 1.0 / den
    return [e * inv for e in es], top + jnp.log2(den)


def merge_tails(tails, t_ref):
    shares, lse = merge_weights([t[0][0] for t in tails])
    _, lse_other = merge_weights([t[0][1] for t in tails])
    dec_shares, dec_lse = merge_weights([t[2] for t in tails])
    dec = sum(t[1] * column(u)[0:STEPR] for t, u in zip(tails, dec_shares))
    put_tail(t_ref, (lse, lse_other), dec, dec_lse)
    return shares, (lse, lse_other), dec, dec_lse


def put_shares(w_ref, shares):
    for n, share in enumerate(shares):
        w_ref[0:LR, n, :] = share
        w_ref[LR, n, :] = jnp.zeros((HD,), F32)


def mix(pieces, w_ref, owner):
    first = owner * ROWS
    both = jnp.concatenate([w_ref[first // HD], w_ref[first // HD + 1]], axis=1)
    own = pltpu.roll(both, (2 * HD - first % HD) % (2 * HD), 1)[:, 0:HD]
    return sum(piece.astype(F32) * column(own[n : n + 1])[0:ROWS] for n, piece in enumerate(pieces))


def pair_kernel(info_ref, a_ref, b_ref, lo_ref, la_ref, da_ref, sb_ref, m_ref, t_ref):
    mine = ((la_ref[...], lo_ref[...]), da_ref[0:STEPR, :], da_ref[STEPR : STEPR + 1, :])
    small = sb_ref[...]
    lse_b, lse_p = small[0:LR], small[16 : 16 + LR]
    theirs = ((lse_b, lse_p), small[32 : 32 + STEPR], small[32 + STEPR : 33 + STEPR])
    (wa, wb), _, _, _ = merge_tails([mine, theirs], t_ref)
    tail = t_ref[...].astype(BF)
    for s in range(NQ):
        m_ref[s, QROWS:, :] = tail
    zl = info_ref[2] % NQ
    for g in range(LR):
        rows = slice(g * HD, (g + 1) * HD)
        a, b = a_ref[rows, :].astype(F32), b_ref[rows, :].astype(F32)
        mixed = (a * column(wa[g : g + 1]) + b * column(wb[g : g + 1])).astype(BF)
        for j in range(0, HD, 32):
            n, at = divmod(g * HD + j, ROWS)
            at += n // NQ * ROWS
            m_ref[zl ^ (n % NQ), at : at + 32, :] = mixed[j : j + 32]


def pair_merge(info, *parts):
    return pl.pallas_call(
        pair_kernel,
        out_shape=jax.ShapeDtypeStruct((NQ, QROWS + TAIL, HD), BF),
        in_specs=[pl.BlockSpec(memory_space=pltpu.SMEM)] + [pl.BlockSpec(memory_space=pltpu.VMEM)] * 6,
        out_specs=pl.BlockSpec(memory_space=pltpu.VMEM),
        scratch_shapes=[pltpu.VMEM((TAIL, HD), F32)],
        compiler_params=params(),
        name="pair_merge",
    )(info, *parts)


def quad_kernel(info_ref, a_ref, b_ref, c_ref, d_ref, z_ref, t_ref, w_ref):
    refs = (a_ref, b_ref, c_ref, d_ref)
    shares, _, _, _ = merge_tails([get_tail(ref[QROWS:, :]) for ref in refs], t_ref)
    put_shares(w_ref, shares)
    tail = t_ref[...].astype(BF)
    zl, zh = info_ref[2] % NQ, info_ref[2] // NQ
    for k in range(NZ // NQ):
        rows = slice(k * ROWS, (k + 1) * ROWS)
        z_ref[zh ^ k, 0:ROWS, :] = mix([ref[rows, :] for ref in refs], w_ref, NQ * k + zl).astype(BF)
        z_ref[k, ROWS:, :] = tail


def quad_merge(info, parts):
    return pl.pallas_call(
        quad_kernel,
        out_shape=jax.ShapeDtypeStruct((NZ // NQ, ROWS + TAIL, HD), BF),
        in_specs=[pl.BlockSpec(memory_space=pltpu.SMEM)] + [pl.BlockSpec(memory_space=pltpu.VMEM)] * 4,
        out_specs=pl.BlockSpec(memory_space=pltpu.VMEM),
        scratch_shapes=[pltpu.VMEM((TAIL, HD), F32), pltpu.VMEM((LR + 1, 8, HD), F32)],
        compiler_params=params(),
        cost_estimate=pl.CostEstimate(flops=100000000000, bytes_accessed=1 << 20, transcendentals=0),
        name="quad_merge",
    )(info, *parts)


def final_kernel(info_ref, a_ref, b_ref, c_ref, d_ref, q_ref, nk_ref, nv_ref, after_ref, slab_ref, lse_ref, step_ref, t_ref, w_ref):
    refs = (a_ref, b_ref, c_ref, d_ref)
    tails = [get_tail(ref[ROWS:, :]) for ref in refs]
    shares, lses, dec, dec_lse = merge_tails(tails, t_ref)
    lse_ref[0:LR, :] = lses[0]
    lse_ref[LR:, :] = lses[1]
    put_shares(w_ref, shares)
    slab_ref[...] = mix([ref[0:ROWS, :] for ref in refs], w_ref, info_ref[2]).astype(BF)
    fresh = scores_t(nk_ref[...], q_ref[...]) * C2
    lane = lax.broadcasted_iota(jnp.int32, (1, HD), 1)
    second = jnp.where(lane % 2 == 1, fresh[1:2], NEG)
    (kept, new_0, new_1), _ = merge_weights([dec_lse, fresh[0:1], second])
    nv = nv_ref[...].astype(F32)
    out = dec * column(kept)[0:STEPR]
    out = out + column(new_0)[0:STEPR] * nv[0:1] + column(new_1)[0:STEPR] * nv[1:2]
    step_ref[...] = out.astype(BF)


def final_merge(info, parts, q, nk, nv, after):
    return pl.pallas_call(
        final_kernel,
        out_shape=(
            jax.ShapeDtypeStruct((ROWS, HD), BF),
            jax.ShapeDtypeStruct((2 * LR, HD), F32),
            jax.ShapeDtypeStruct((STEPR, HD), BF),
        ),
        in_specs=[pl.BlockSpec(memory_space=pltpu.SMEM)] + [pl.BlockSpec(memory_space=pltpu.VMEM)] * 8,
        out_specs=[pl.BlockSpec(memory_space=pltpu.VMEM)] * 3,
        scratch_shapes=[pltpu.VMEM((TAIL, HD), F32), pltpu.VMEM((LR + 1, 8, HD), F32)],
        compiler_params=params(),
        name="final_merge",
    )(info, *parts, q, nk, nv, after)


def heavy_kernel(info_ref, q_ref, k_ref, lse_ref, h_ref, acc_ref):
    i = pl.program_id(0)

    @pl.when(i == 0)
    def _():
        acc_ref[...] = jnp.zeros_like(acc_ref)

    q = q_ref[...]
    per = RB // HD
    other = i // NRB
    lse = jnp.concatenate([lse_ref[pl.ds(i * per + j, 1), :] for j in range(per)], axis=1)
    for c in range(CTXL // SLAB):
        keys = slice(c * SLAB, (c + 1) * SLAB)
        s = scores_t(k_ref[0, keys, :], q)
        if c == CTXL // SLAB - 1:
            s = masked_tail(info_ref, info_ref[1] ^ other, i - other * NRB, s)
        w = jnp.exp2(s * C2 - lse)
        acc_ref[keys, :] += (w[:, 0:128] + w[:, 128:256]) + (w[:, 256:384] + w[:, 384:512])

    @pl.when(i == 2 * NRB - 1)
    def _():
        for t in range(CTXL // HD):
            at = slice(t * HD, (t + 1) * HD)
            sums = jnp.sum(acc_ref[at, :].T, axis=0, keepdims=True)
            h_ref[:, at] = sums * (NCTX * CTXL / (12 * SLAB))


def heavy(info, q, kv, lse):
    return pl.pallas_call(
        heavy_kernel,
        out_shape=jax.ShapeDtypeStruct((1, CTXL), F32),
        grid=(2 * NRB,),
        in_specs=[
            pl.BlockSpec(memory_space=pltpu.SMEM),
            pl.BlockSpec((RB, HD), lambda i: (i, 0)),
            pl.BlockSpec((1, CTXL, HD), lambda i: (0, 0, 0)),
            pl.BlockSpec((2 * LR, HD), lambda i: (0, 0)),
        ],
        out_specs=pl.BlockSpec((1, CTXL), lambda i: (0, 0)),
        scratch_shapes=[pltpu.VMEM((CTXL, HD), F32)],
        compiler_params=params(),
        cost_estimate=pl.CostEstimate(
            flops=4 * HALF * CTXL * HD, bytes_accessed=CTXL * HD * 2, transcendentals=2 * HALF * CTXL
        ),
        name="heavy_columns",
    )(info, q, kv, lse)


def pack_kernel(spans, pick_ref, kv_ref, after_ref, out_ref, sems):
    copies, at = [], 0
    for n, (part, start, count) in enumerate(spans):
        for d in range(NCTX):
            source = kv_ref.at[part, pick_ref[d], start : start + count]
            copies.append(pltpu.make_async_copy(source, out_ref.at[d, at : at + count], sems.at[n, d]))
        at += count
    for copy in copies:
        copy.start()
    for copy in copies:
        copy.wait()


def pack(spans, pick, blocks, after):
    return pl.pallas_call(
        functools.partial(pack_kernel, spans),
        out_shape=jax.ShapeDtypeStruct((NCTX, sum(span[2] for span in spans), HD), BF),
        in_specs=[pl.BlockSpec(memory_space=pltpu.SMEM)] + [pl.BlockSpec(memory_space=pltpu.VMEM)] * 2,
        out_specs=pl.BlockSpec(memory_space=pl.ANY),
        scratch_shapes=[pltpu.SemaphoreType.DMA((len(spans), NCTX))],
        compiler_params=params(),
        name="pack_blocks",
    )(pick, blocks, after)


def held_kernel(x_ref, after_ref, out_ref):
    out_ref[...] = x_ref[...]


def held(x, other):
    return pl.pallas_call(
        held_kernel,
        out_shape=jax.ShapeDtypeStruct(x.shape, x.dtype),
        compiler_params=params(),
        name="held",
    )(x, other)


def after_kernel(x_ref, after_ref, out_ref):
    del x_ref, after_ref, out_ref


def after(x, other):
    return pl.pallas_call(
        after_kernel,
        out_shape=jax.ShapeDtypeStruct(x.shape, x.dtype),
        in_specs=[pl.BlockSpec(memory_space=pl.ANY), pl.BlockSpec(memory_space=pltpu.VMEM)],
        out_specs=pl.BlockSpec(memory_space=pl.ANY),
        input_output_aliases={0: 0},
        name="after",
    )(x, other)


def select_kernel(src_ref, a_ref, b_ref, out_ref, sems):
    copies = []
    for r in range(SLOTS):
        at = src_ref[r]
        for n, (source, target) in enumerate((
            (a_ref.at[at, 0:BLK], out_ref.at[0, r]),
            (a_ref.at[at, BLK : BLK + FIRST], out_ref.at[1, r, 0:FIRST]),
            (b_ref.at[at], out_ref.at[1, r, FIRST:BLK]),
        )):
            copies.append(pltpu.make_async_copy(source, target, sems.at[n, r]))
    for copy in copies:
        copy.start()
    for copy in copies:
        copy.wait()


def select(source, first, second):
    return pl.pallas_call(
        select_kernel,
        out_shape=jax.ShapeDtypeStruct((2, SLOTS, BLK, HD), BF),
        in_specs=[pl.BlockSpec(memory_space=pltpu.SMEM)] + [pl.BlockSpec(memory_space=pl.ANY)] * 2,
        out_specs=pl.BlockSpec(memory_space=pltpu.VMEM),
        scratch_shapes=[pltpu.SemaphoreType.DMA((3, SLOTS))],
        compiler_params=params(),
        name="select_slots",
    )(source, first, second)


def spread_kernel(q_ref, out_ref):
    for n in range(NZ // 2):
        out_ref[n] = q_ref[...]


def spread(q):
    return pl.pallas_call(
        spread_kernel,
        out_shape=jax.ShapeDtypeStruct((NZ // 2, ROWS, HD), BF),
        compiler_params=params(),
        name="spread_queries",
    )(q)


SWAP = [(0, 1), (1, 0)]


CTX = ("xl", "zh", "zm", "zp")
BLOCKS = ("zh", "zm", "zp", "xl")


def local(slab_query, kv_cache, kept_list, decode_place, step_query, step_cache):
    grp = lax.axis_index("grp")
    xl = lax.axis_index("xl")
    zp = lax.axis_index("zp")
    z = lax.axis_index("zh") * NQ + lax.axis_index("zm") * 2 + zp
    ctx = xl * NZ + z
    per_dev = CTXL // BLK

    kept = lax.dynamic_index_in_dim(kept_list, 1 - grp, 0, keepdims=False)[0]
    place = lax.dynamic_index_in_dim(decode_place, 1 - grp, 0, keepdims=False)[0]
    slots = jnp.arange(NCTX, dtype=jnp.int32)
    lanes = slots % 2 * NZ + slots // 2
    offset = kept - ctx * per_dev
    mine = (offset >= 0) & (offset < per_dev)
    hit = mine[None, :] & (place[None, :] == lanes[:, None])
    pick = jnp.clip(jnp.sum(jnp.where(hit, offset[None, :], 0), axis=1), 0, per_dev - 1)
    flags = jnp.sum(
        (offset[None, :] == jnp.arange(per_dev, dtype=jnp.int32)[:, None]).astype(jnp.int32), axis=1
    )
    here = (place == ctx).reshape(SLOTS, NCTX)
    owner = jnp.sum(jnp.where(here, kept.reshape(SLOTS, NCTX) // per_dev, 0), axis=1)
    source = jnp.clip(owner % NZ * 2 + owner // NZ, 0, NCTX - 1)
    info = jnp.stack([ctx, xl, z]).astype(jnp.int32)

    q = jnp.transpose(slab_query[0, :, 0], (1, 0, 2)).reshape(ROWS, HD)
    kv = kv_cache[0, :, :, 0]
    steps = jnp.transpose(step_query[0, :, 0], (1, 0, 2)).reshape(STEPR, HD)
    steps = jnp.pad(steps, ((0, HD - STEPR), (0, 0)))
    new = jnp.pad(step_cache[0, :, :, 0], ((0, 0), (0, 14), (0, 0)))

    kv_decode = lax.ppermute(kv, "grp", SWAP)
    blocks = kv_decode.reshape(2, per_dev, BLK, HD)
    q_same = lax.all_to_all(spread(q), ("zh", "zm"), 0, 0, tiled=True)
    packed = pack(((0, 0, BLK), (1, 0, FIRST)), pick, blocks, steps[0:16])
    q_next = lax.ppermute(held(q_same, packed[0, 0:16]), "zp", SWAP)
    even, odd = jnp.where(zp == 0, q_same, q_next), jnp.where(zp == 0, q_next, q_same)
    q_own = jnp.stack([even, odd], axis=1).reshape(HALF, HD)
    dec = decode_partial(flags, steps, kv_decode)

    keys = lax.all_to_all(packed, BLOCKS, 0, 0, tiled=True)
    q_other = lax.ppermute(q_own, "xl", SWAP)
    part_own, lse_own = flash(0, info, q_own, kv, dec[0:8])
    part_other, lse_other = flash(1, info, q_other, kv, lse_own[0:8])
    blank = jnp.zeros((16 - LR, HD), F32)
    small = lax.ppermute(jnp.concatenate([lse_other, blank, lse_own, blank, dec], axis=0), "xl", SWAP)
    part_beside = lax.ppermute(part_other, "xl", SWAP)
    parts = pair_merge(info, part_own, part_beside, lse_other, lse_own, dec, small)
    near = [lax.ppermute(parts[s], ("zm", "zp"), [(i, i ^ s) for i in range(NQ)]) for s in range(1, NQ)]
    rest = pack(((1, FIRST, BLK - FIRST),), pick, blocks, parts[0, 0:16])
    values = lax.all_to_all(after(rest, keys[0, 0:16]), BLOCKS, 0, 0, tiled=True)
    merged = quad_merge(info, [parts[0]] + near)
    far = [lax.ppermute(merged[s], "zh", [(i, i ^ s) for i in range(NZ // NQ)]) for s in range(1, NZ // NQ)]
    paged = select(source, keys, values)
    slab, lse, step = final_merge(info, [merged[0]] + far, steps, new[0], new[1], paged[0, 0, 0:16])
    columns = heavy(info, jnp.concatenate([q_own, q_other], axis=0), kv, lse)

    slab_out = jnp.transpose(slab.reshape(12, 8, HD), (1, 0, 2))[None, :, None]
    step_out = jnp.transpose(step.reshape(12, 2, HD), (1, 0, 2))[None, :, None]
    return (slab_out, columns[None], paged[None, None], step_out)


def solution(mesh):
    split = Mesh(mesh.devices.reshape(2, 2, NZ // NQ, 2, 2, 8), ("grp", "xl", "zh", "zm", "zp", "kvh"))
    return jax.shard_map(
        local,
        mesh=split,
        in_specs=(
            P("grp", CTX, "kvh", None, None),
            P("grp", None, CTX, "kvh", None),
            P(None, "kvh", None),
            P(None, "kvh", None),
            P("grp", None, "kvh", None, None),
            P("grp", None, None, "kvh", None),
        ),
        out_specs=(
            P("grp", CTX, "kvh", None, None),
            P("grp", "kvh", CTX),
            P("grp", "kvh", None, CTX, None, None),
            P("grp", None, "kvh", None, None),
        ),
        check_vma=False,
    )
```

```python
import functools
import math

import jax
import jax.numpy as jnp
from jax import lax
from jax.experimental import pallas as pl
from jax.experimental.pallas import tpu as pltpu
from jax.sharding import Mesh
from jax.sharding import PartitionSpec as P

BLK = 128
HD = 128
NZ = 16
NCTX = 32
ROWS = 96
HALF = NZ * ROWS
CTXL = 2048
SLAB = 256
RB = 512
NRB = HALF // RB
SLOTS = 12
STEPR = 24
NEG = -1e30
C2 = math.log2(math.e) / math.sqrt(HD)
BF = jnp.bfloat16
F32 = jnp.float32

LR = HALF // HD
NQ = 4
QROWS = NZ // NQ * ROWS
FIRST = 32
DECR = 6 * LR
DSTAT = DECR + STEPR
TAIL = 112
DEC = 32


def params(mib=40):
    return pltpu.CompilerParams(vmem_limit_bytes=mib * 1024 * 1024)


def parts_of(x):
    hi = x.astype(BF).astype(F32)
    mid = (x - hi).astype(BF).astype(F32)
    return hi, mid, x - hi - mid


def column(row):
    return jnp.broadcast_to(row, (128, 128)).T


def scores_t(k, q):
    return lax.dot_general(k, q, (((1,), (1,)), ((), ())), preferred_element_type=F32)


def masked_tail(info_ref, half, i, tail):
    key = lax.broadcasted_iota(jnp.int32, tail.shape, 0)
    row = lax.broadcasted_iota(jnp.int32, tail.shape, 1) + i * RB
    token = half * (SLAB // 2) + (row // ROWS) * 8 + row % 8
    seen = (key <= token) | (info_ref[0] < NCTX - 1)
    return jnp.where(seen, tail, NEG)


def fill_vt(v, vt_ref):
    vt_ref[0:HD, :] = v.astype(F32).T.astype(BF)
    vt_ref[HD:, :] = jnp.ones((16, CTXL), BF)


def put_tail(t_ref, lses, dec, dec_lse):
    for m, lse in enumerate(lses):
        for n, part in enumerate(parts_of(lse)):
            t_ref[(3 * m + n) * LR : (3 * m + n + 1) * LR, :] = part
    t_ref[DECR:DSTAT, :] = dec
    for n, part in enumerate(parts_of(dec_lse)):
        t_ref[DSTAT + n : DSTAT + n + 1, :] = part
    t_ref[DSTAT + 3 :, :] = jnp.zeros((TAIL - DSTAT - 3, HD), F32)


def get_tail(t):
    t = t.astype(F32)
    lses = [sum(t[(3 * m + n) * LR : (3 * m + n + 1) * LR] for n in range(3)) for m in range(2)]
    dec_lse = t[DSTAT : DSTAT + 1] + t[DSTAT + 1 : DSTAT + 2] + t[DSTAT + 2 : DSTAT + 3]
    return lses, t[DECR:DSTAT], dec_lse


def flash_kernel(other, info_ref, q_ref, k_ref, v_ref, after_ref, x_ref, lse_ref, vt_ref, s_ref):
    i = pl.program_id(0)

    @pl.when(i == 0)
    def _():
        fill_vt(v_ref[0], vt_ref)

    s_ref[...] = scores_t(k_ref[0], q_ref[...])
    s_ref[CTXL - SLAB :, :] = masked_tail(info_ref, info_ref[1] ^ other, i, s_ref[CTXL - SLAB :, :])
    top = jnp.max(s_ref[...], axis=0, keepdims=True)
    p = jnp.exp2((s_ref[...] - top) * C2).astype(BF)
    acc = jnp.dot(vt_ref[...], p, preferred_element_type=F32)
    mass = acc[HD : HD + 1]
    x_ref[...] = (acc[0:HD] * (1.0 / mass)).T.astype(BF)
    lse = top * C2 + jnp.log2(mass)
    for j in range(RB // HD):
        lse_ref[pl.ds(i * (RB // HD) + j, 1), :] = lse[:, j * HD : (j + 1) * HD]


def flash(other, info, q, kv, after):
    return pl.pallas_call(
        functools.partial(flash_kernel, other),
        out_shape=(jax.ShapeDtypeStruct((HALF, HD), BF), jax.ShapeDtypeStruct((LR, HD), F32)),
        grid=(NRB,),
        in_specs=[
            pl.BlockSpec(memory_space=pltpu.SMEM),
            pl.BlockSpec((RB, HD), lambda i: (i, 0)),
            pl.BlockSpec((1, CTXL, HD), lambda i: (0, 0, 0)),
            pl.BlockSpec((1, CTXL, HD), lambda i: (1, 0, 0)),
            pl.BlockSpec((8, HD), lambda i: (0, 0)),
        ],
        out_specs=(pl.BlockSpec((RB, HD), lambda i: (i, 0)), pl.BlockSpec((LR, HD), lambda i: (0, 0))),
        scratch_shapes=[pltpu.VMEM((HD + 16, CTXL), BF), pltpu.VMEM((CTXL, RB), F32)],
        compiler_params=params(),
        cost_estimate=pl.CostEstimate(
            flops=20000000000, bytes_accessed=2 * CTXL * HD * 2, transcendentals=HALF * CTXL
        ),
        name="slab_partial",
    )(info, q, kv, kv, after)


def decode_kernel(flag_ref, q_ref, k_ref, v_ref, d_ref, vt_ref, s_ref):
    fill_vt(v_ref[0], vt_ref)
    for b in range(CTXL // BLK):
        s = scores_t(k_ref[0, b * BLK : (b + 1) * BLK, :], q_ref[...])
        kept = jnp.broadcast_to(flag_ref[b], s.shape) > 0
        s_ref[b * BLK : (b + 1) * BLK, :] = jnp.where(kept, s, NEG)
    top = jnp.max(s_ref[...], axis=0, keepdims=True)
    p = jnp.exp2((s_ref[...] - top) * C2).astype(BF)
    acc = jnp.dot(vt_ref[...], p, preferred_element_type=F32)
    mass = acc[HD : HD + 1]
    out = (acc[0:HD] * (1.0 / mass)).T
    lse = jnp.maximum(top * C2 + jnp.log2(mass), NEG)
    d_ref[...] = jnp.zeros_like(d_ref)
    d_ref[0:STEPR, :] = out[0:STEPR]
    d_ref[STEPR : STEPR + 1, :] = lse


def decode_partial(flags, q, kv):
    return pl.pallas_call(
        decode_kernel,
        out_shape=jax.ShapeDtypeStruct((DEC, HD), F32),
        grid=(1,),
        in_specs=[
            pl.BlockSpec(memory_space=pltpu.SMEM),
            pl.BlockSpec((HD, HD), lambda i: (0, 0)),
            pl.BlockSpec((1, CTXL, HD), lambda i: (0, 0, 0)),
            pl.BlockSpec((1, CTXL, HD), lambda i: (1, 0, 0)),
        ],
        out_specs=pl.BlockSpec((DEC, HD), lambda i: (0, 0)),
        scratch_shapes=[
            pltpu.VMEM((HD + 16, CTXL), BF),
            pltpu.VMEM((CTXL, HD), F32),
        ],
        compiler_params=params(),
        name="decode_partial",
    )(flags, q, kv, kv)


def merge_weights(lses):
    top = lses[0]
    for x in lses[1:]:
        top = jnp.maximum(top, x)
    es = [jnp.exp2(x - top) for x in lses]
    den = es[0]
    for e in es[1:]:
        den = den + e
    inv = 1.0 / den
    return [e * inv for e in es], top + jnp.log2(den)


def merge_tails(tails, t_ref):
    shares, lse = merge_weights([t[0][0] for t in tails])
    _, lse_other = merge_weights([t[0][1] for t in tails])
    dec_shares, dec_lse = merge_weights([t[2] for t in tails])
    dec = sum(t[1] * column(u)[0:STEPR] for t, u in zip(tails, dec_shares))
    put_tail(t_ref, (lse, lse_other), dec, dec_lse)
    return shares, (lse, lse_other), dec, dec_lse


def put_shares(w_ref, shares):
    for n, share in enumerate(shares):
        w_ref[0:LR, n, :] = share
        w_ref[LR, n, :] = jnp.zeros((HD,), F32)


def mix(pieces, w_ref, owner):
    first = owner * ROWS
    both = jnp.concatenate([w_ref[first // HD], w_ref[first // HD + 1]], axis=1)
    own = pltpu.roll(both, (2 * HD - first % HD) % (2 * HD), 1)[:, 0:HD]
    return sum(piece.astype(F32) * column(own[n : n + 1])[0:ROWS] for n, piece in enumerate(pieces))


def pair_kernel(info_ref, a_ref, b_ref, lo_ref, la_ref, da_ref, sb_ref, m_ref, t_ref):
    mine = ((la_ref[...], lo_ref[...]), da_ref[0:STEPR, :], da_ref[STEPR : STEPR + 1, :])
    small = sb_ref[...]
    lse_b, lse_p = small[0:LR], small[16 : 16 + LR]
    theirs = ((lse_b, lse_p), small[32 : 32 + STEPR], small[32 + STEPR : 33 + STEPR])
    (wa, wb), _, _, _ = merge_tails([mine, theirs], t_ref)
    tail = t_ref[...].astype(BF)
    for s in range(NQ):
        m_ref[s, QROWS:, :] = tail
    zl = info_ref[2] % NQ
    for g in range(LR):
        rows = slice(g * HD, (g + 1) * HD)
        a, b = a_ref[rows, :].astype(F32), b_ref[rows, :].astype(F32)
        mixed = (a * column(wa[g : g + 1]) + b * column(wb[g : g + 1])).astype(BF)
        for j in range(0, HD, 32):
            n, at = divmod(g * HD + j, ROWS)
            at += n // NQ * ROWS
            m_ref[zl ^ (n % NQ), at : at + 32, :] = mixed[j : j + 32]


def pair_merge(info, *parts):
    return pl.pallas_call(
        pair_kernel,
        out_shape=jax.ShapeDtypeStruct((NQ, QROWS + TAIL, HD), BF),
        in_specs=[pl.BlockSpec(memory_space=pltpu.SMEM)] + [pl.BlockSpec(memory_space=pltpu.VMEM)] * 6,
        out_specs=pl.BlockSpec(memory_space=pltpu.VMEM),
        scratch_shapes=[pltpu.VMEM((TAIL, HD), F32)],
        compiler_params=params(),
        name="pair_merge",
    )(info, *parts)


def quad_kernel(info_ref, a_ref, b_ref, c_ref, d_ref, z_ref, t_ref, w_ref):
    refs = (a_ref, b_ref, c_ref, d_ref)
    shares, _, _, _ = merge_tails([get_tail(ref[QROWS:, :]) for ref in refs], t_ref)
    put_shares(w_ref, shares)
    tail = t_ref[...].astype(BF)
    zl, zh = info_ref[2] % NQ, info_ref[2] // NQ
    for k in range(NZ // NQ):
        rows = slice(k * ROWS, (k + 1) * ROWS)
        z_ref[zh ^ k, 0:ROWS, :] = mix([ref[rows, :] for ref in refs], w_ref, NQ * k + zl).astype(BF)
        z_ref[k, ROWS:, :] = tail


def quad_merge(info, parts):
    return pl.pallas_call(
        quad_kernel,
        out_shape=jax.ShapeDtypeStruct((NZ // NQ, ROWS + TAIL, HD), BF),
        in_specs=[pl.BlockSpec(memory_space=pltpu.SMEM)] + [pl.BlockSpec(memory_space=pltpu.VMEM)] * 4,
        out_specs=pl.BlockSpec(memory_space=pltpu.VMEM),
        scratch_shapes=[pltpu.VMEM((TAIL, HD), F32), pltpu.VMEM((LR + 1, 8, HD), F32)],
        compiler_params=params(),
        cost_estimate=pl.CostEstimate(flops=100000000000, bytes_accessed=1 << 20, transcendentals=0),
        name="quad_merge",
    )(info, *parts)


def final_kernel(info_ref, a_ref, b_ref, c_ref, d_ref, q_ref, nk_ref, nv_ref, after_ref, slab_ref, lse_ref, step_ref, t_ref, w_ref):
    refs = (a_ref, b_ref, c_ref, d_ref)
    tails = [get_tail(ref[ROWS:, :]) for ref in refs]
    shares, lses, dec, dec_lse = merge_tails(tails, t_ref)
    lse_ref[0:LR, :] = lses[0]
    lse_ref[LR:, :] = lses[1]
    put_shares(w_ref, shares)
    slab_ref[...] = mix([ref[0:ROWS, :] for ref in refs], w_ref, info_ref[2]).astype(BF)
    fresh = scores_t(nk_ref[...], q_ref[...]) * C2
    lane = lax.broadcasted_iota(jnp.int32, (1, HD), 1)
    second = jnp.where(lane % 2 == 1, fresh[1:2], NEG)
    (kept, new_0, new_1), _ = merge_weights([dec_lse, fresh[0:1], second])
    nv = nv_ref[...].astype(F32)
    out = dec * column(kept)[0:STEPR]
    out = out + column(new_0)[0:STEPR] * nv[0:1] + column(new_1)[0:STEPR] * nv[1:2]
    step_ref[...] = out.astype(BF)


def final_merge(info, parts, q, nk, nv, after):
    return pl.pallas_call(
        final_kernel,
        out_shape=(
            jax.ShapeDtypeStruct((ROWS, HD), BF),
            jax.ShapeDtypeStruct((2 * LR, HD), F32),
            jax.ShapeDtypeStruct((STEPR, HD), BF),
        ),
        in_specs=[pl.BlockSpec(memory_space=pltpu.SMEM)] + [pl.BlockSpec(memory_space=pltpu.VMEM)] * 8,
        out_specs=[pl.BlockSpec(memory_space=pltpu.VMEM)] * 3,
        scratch_shapes=[pltpu.VMEM((TAIL, HD), F32), pltpu.VMEM((LR + 1, 8, HD), F32)],
        compiler_params=params(),
        name="final_merge",
    )(info, *parts, q, nk, nv, after)


def heavy_kernel(info_ref, q_ref, k_ref, lse_ref, h_ref, acc_ref):
    i = pl.program_id(0)

    @pl.when(i == 0)
    def _():
        acc_ref[...] = jnp.zeros_like(acc_ref)

    q = q_ref[...]
    per = RB // HD
    other = i // NRB
    lse = jnp.concatenate([lse_ref[pl.ds(i * per + j, 1), :] for j in range(per)], axis=1)
    for c in range(CTXL // SLAB):
        keys = slice(c * SLAB, (c + 1) * SLAB)
        s = scores_t(k_ref[0, keys, :], q)
        if c == CTXL // SLAB - 1:
            s = masked_tail(info_ref, info_ref[1] ^ other, i - other * NRB, s)
        w = jnp.exp2(s * C2 - lse)
        acc_ref[keys, :] += (w[:, 0:128] + w[:, 128:256]) + (w[:, 256:384] + w[:, 384:512])

    @pl.when(i == 2 * NRB - 1)
    def _():
        for t in range(CTXL // HD):
            at = slice(t * HD, (t + 1) * HD)
            sums = jnp.sum(acc_ref[at, :].T, axis=0, keepdims=True)
            h_ref[:, at] = sums * (NCTX * CTXL / (12 * SLAB))


def heavy(info, q, kv, lse):
    return pl.pallas_call(
        heavy_kernel,
        out_shape=jax.ShapeDtypeStruct((1, CTXL), F32),
        grid=(2 * NRB,),
        in_specs=[
            pl.BlockSpec(memory_space=pltpu.SMEM),
            pl.BlockSpec((RB, HD), lambda i: (i, 0)),
            pl.BlockSpec((1, CTXL, HD), lambda i: (0, 0, 0)),
            pl.BlockSpec((2 * LR, HD), lambda i: (0, 0)),
        ],
        out_specs=pl.BlockSpec((1, CTXL), lambda i: (0, 0)),
        scratch_shapes=[pltpu.VMEM((CTXL, HD), F32)],
        compiler_params=params(60),
        cost_estimate=pl.CostEstimate(
            flops=4 * HALF * CTXL * HD, bytes_accessed=CTXL * HD * 2, transcendentals=2 * HALF * CTXL
        ),
        name="heavy_columns",
    )(info, q, kv, lse)


def pack_kernel(spans, pick_ref, kv_ref, after_ref, out_ref, sems):
    copies, at = [], 0
    for n, (part, start, count) in enumerate(spans):
        for d in range(NCTX):
            source = kv_ref.at[part, pick_ref[d], start : start + count]
            copies.append(pltpu.make_async_copy(source, out_ref.at[d, at : at + count], sems.at[n, d]))
        at += count
    for copy in copies:
        copy.start()
    for copy in copies:
        copy.wait()


def pack(spans, pick, blocks, after):
    return pl.pallas_call(
        functools.partial(pack_kernel, spans),
        out_shape=jax.ShapeDtypeStruct((NCTX, sum(span[2] for span in spans), HD), BF),
        in_specs=[pl.BlockSpec(memory_space=pltpu.SMEM)] + [pl.BlockSpec(memory_space=pltpu.VMEM)] * 2,
        out_specs=pl.BlockSpec(memory_space=pl.ANY),
        scratch_shapes=[pltpu.SemaphoreType.DMA((len(spans), NCTX))],
        compiler_params=params(),
        name="pack_blocks",
    )(pick, blocks, after)


def held_kernel(x_ref, after_ref, out_ref):
    out_ref[...] = x_ref[...]


def held(x, other):
    return pl.pallas_call(
        held_kernel,
        out_shape=jax.ShapeDtypeStruct(x.shape, x.dtype),
        compiler_params=params(),
        name="held",
    )(x, other)


def picked_kernel(x_ref, out_ref):
    out_ref[...] = x_ref[...]


def picked(x):
    return pl.pallas_call(
        picked_kernel,
        out_shape=jax.ShapeDtypeStruct(x.shape, x.dtype),
        compiler_params=params(),
        cost_estimate=pl.CostEstimate(flops=1000000000, bytes_accessed=4096, transcendentals=0),
        name="picked",
    )(x)


def after_kernel(x_ref, after_ref, out_ref):
    del x_ref, after_ref, out_ref


def after(x, other):
    return pl.pallas_call(
        after_kernel,
        out_shape=jax.ShapeDtypeStruct(x.shape, x.dtype),
        in_specs=[pl.BlockSpec(memory_space=pl.ANY), pl.BlockSpec(memory_space=pltpu.VMEM)],
        out_specs=pl.BlockSpec(memory_space=pl.ANY),
        input_output_aliases={0: 0},
        name="after",
    )(x, other)


def select_kernel(src_ref, a_ref, b_ref, out_ref, sems):
    copies = []
    for r in range(SLOTS):
        at = src_ref[r]
        for n, (source, target) in enumerate((
            (a_ref.at[at, 0:BLK], out_ref.at[0, r]),
            (a_ref.at[at, BLK : BLK + FIRST], out_ref.at[1, r, 0:FIRST]),
            (b_ref.at[at], out_ref.at[1, r, FIRST:BLK]),
        )):
            copies.append(pltpu.make_async_copy(source, target, sems.at[n, r]))
    for copy in copies:
        copy.start()
    for copy in copies:
        copy.wait()


def select(source, first, second):
    return pl.pallas_call(
        select_kernel,
        out_shape=jax.ShapeDtypeStruct((2, SLOTS, BLK, HD), BF),
        in_specs=[pl.BlockSpec(memory_space=pltpu.SMEM)] + [pl.BlockSpec(memory_space=pl.ANY)] * 2,
        out_specs=pl.BlockSpec(memory_space=pltpu.VMEM),
        scratch_shapes=[pltpu.SemaphoreType.DMA((3, SLOTS))],
        compiler_params=params(),
        name="select_slots",
    )(source, first, second)


def spread_kernel(q_ref, out_ref):
    for n in range(NZ // 2):
        out_ref[n] = q_ref[...]


def spread(q):
    return pl.pallas_call(
        spread_kernel,
        out_shape=jax.ShapeDtypeStruct((NZ // 2, ROWS, HD), BF),
        compiler_params=params(),
        name="spread_queries",
    )(q)


SWAP = [(0, 1), (1, 0)]


CTX = ("xl", "zh", "zm", "zp")
BLOCKS = ("zh", "zm", "zp", "xl")


def local(slab_query, kv_cache, kept_list, decode_place, step_query, step_cache):
    grp = lax.axis_index("grp")
    xl = lax.axis_index("xl")
    zp = lax.axis_index("zp")
    z = lax.axis_index("zh") * NQ + lax.axis_index("zm") * 2 + zp
    ctx = xl * NZ + z
    per_dev = CTXL // BLK

    kept = lax.dynamic_index_in_dim(kept_list, 1 - grp, 0, keepdims=False)[0]
    place = lax.dynamic_index_in_dim(decode_place, 1 - grp, 0, keepdims=False)[0]
    slots = jnp.arange(NCTX, dtype=jnp.int32)
    lanes = slots % 2 * NZ + slots // 2
    offset = kept - ctx * per_dev
    mine = (offset >= 0) & (offset < per_dev)
    hit = mine[None, :] & (place[None, :] == lanes[:, None])
    pick = jnp.clip(jnp.sum(jnp.where(hit, offset[None, :], 0), axis=1), 0, per_dev - 1)
    flags = jnp.sum(
        (offset[None, :] == jnp.arange(per_dev, dtype=jnp.int32)[:, None]).astype(jnp.int32), axis=1
    )
    here = (place == ctx).reshape(SLOTS, NCTX)
    owner = jnp.sum(jnp.where(here, kept.reshape(SLOTS, NCTX) // per_dev, 0), axis=1)
    source = jnp.clip(owner % NZ * 2 + owner // NZ, 0, NCTX - 1)
    info = jnp.stack([ctx, xl, z]).astype(jnp.int32)

    q = jnp.transpose(slab_query[0, :, 0], (1, 0, 2)).reshape(ROWS, HD)
    kv = kv_cache[0, :, :, 0]
    steps = jnp.transpose(step_query[0, :, 0], (1, 0, 2)).reshape(STEPR, HD)
    steps = jnp.pad(steps, ((0, HD - STEPR), (0, 0)))
    new = jnp.pad(step_cache[0, :, :, 0], ((0, 0), (0, 14), (0, 0)))

    kv_decode = lax.ppermute(kv, "grp", SWAP)
    blocks = kv_decode.reshape(2, per_dev, BLK, HD)
    q_same = lax.all_to_all(spread(q), ("zh", "zm"), 0, 0, tiled=True)
    pick = picked(pick.reshape(1, NCTX)).reshape(NCTX)
    packed = pack(((0, 0, BLK), (1, 0, FIRST)), pick, blocks, steps[0:16])
    q_next = lax.ppermute(held(q_same, packed[0, 0:16]), "zp", SWAP)
    even, odd = jnp.where(zp == 0, q_same, q_next), jnp.where(zp == 0, q_next, q_same)
    q_own = jnp.stack([even, odd], axis=1).reshape(HALF, HD)
    dec = decode_partial(flags, steps, kv_decode)

    keys = lax.all_to_all(packed, BLOCKS, 0, 0, tiled=True)
    q_other = lax.ppermute(q_own, "xl", SWAP)
    part_own, lse_own = flash(0, info, q_own, kv, dec[0:8])
    part_other, lse_other = flash(1, info, q_other, kv, lse_own[0:8])
    blank = jnp.zeros((16 - LR, HD), F32)
    small = lax.ppermute(jnp.concatenate([lse_other, blank, lse_own, blank, dec], axis=0), "xl", SWAP)
    part_beside = lax.ppermute(part_other, "xl", SWAP)
    parts = pair_merge(info, part_own, part_beside, lse_other, lse_own, dec, small)
    near = [lax.ppermute(parts[s], ("zm", "zp"), [(i, i ^ s) for i in range(NQ)]) for s in range(1, NQ)]
    rest = pack(((1, FIRST, BLK - FIRST),), pick, blocks, parts[0, 0:16])
    values = lax.all_to_all(after(rest, keys[0, 0:16]), BLOCKS, 0, 0, tiled=True)
    merged = quad_merge(info, [parts[0]] + near)
    far = [lax.ppermute(merged[s], "zh", [(i, i ^ s) for i in range(NZ // NQ)]) for s in range(1, NZ // NQ)]
    paged = select(source, keys, values)
    slab, lse, step = final_merge(info, [merged[0]] + far, steps, new[0], new[1], paged[0, 0, 0:16])
    columns = heavy(info, jnp.concatenate([q_own, q_other], axis=0), kv, lse)

    slab_out = jnp.transpose(slab.reshape(12, 8, HD), (1, 0, 2))[None, :, None]
    step_out = jnp.transpose(step.reshape(12, 2, HD), (1, 0, 2))[None, :, None]
    return (slab_out, columns[None], paged[None, None], step_out)


def solution(mesh):
    split = Mesh(mesh.devices.reshape(2, 2, NZ // NQ, 2, 2, 8), ("grp", "xl", "zh", "zm", "zp", "kvh"))
    return jax.shard_map(
        local,
        mesh=split,
        in_specs=(
            P("grp", CTX, "kvh", None, None),
            P("grp", None, CTX, "kvh", None),
            P(None, "kvh", None),
            P(None, "kvh", None),
            P("grp", None, "kvh", None, None),
            P("grp", None, None, "kvh", None),
        ),
        out_specs=(
            P("grp", CTX, "kvh", None, None),
            P("grp", "kvh", CTX),
            P("grp", "kvh", None, CTX, None, None),
            P("grp", None, "kvh", None, None),
        ),
        check_vma=False,
    )
```

```python
import functools
import math

import jax
import jax.numpy as jnp
from jax import lax
from jax.experimental import pallas as pl
from jax.experimental.pallas import tpu as pltpu
from jax.sharding import Mesh
from jax.sharding import PartitionSpec as P

BLK = 128
HD = 128
NZ = 16
NCTX = 32
ROWS = 96
HALF = NZ * ROWS
CTXL = 2048
SLAB = 256
RB = 512
NRB = HALF // RB
SLOTS = 12
STEPR = 24
NEG = -1e30
C2 = math.log2(math.e) / math.sqrt(HD)
BF = jnp.bfloat16
F32 = jnp.float32

LR = HALF // HD
NQ = 4
QROWS = NZ // NQ * ROWS
FIRST = 16
DECR = 6 * LR
DSTAT = DECR + STEPR
TAIL = 112
DEC = 32


def params(mib=40):
    return pltpu.CompilerParams(vmem_limit_bytes=mib * 1024 * 1024)


def parts_of(x):
    hi = x.astype(BF).astype(F32)
    mid = (x - hi).astype(BF).astype(F32)
    return hi, mid, x - hi - mid


def column(row):
    return jnp.broadcast_to(row, (128, 128)).T


def scores_t(k, q):
    return lax.dot_general(k, q, (((1,), (1,)), ((), ())), preferred_element_type=F32)


def masked_tail(info_ref, half, i, tail):
    key = lax.broadcasted_iota(jnp.int32, tail.shape, 0)
    row = lax.broadcasted_iota(jnp.int32, tail.shape, 1) + i * RB
    token = half * (SLAB // 2) + (row // ROWS) * 8 + row % 8
    seen = (key <= token) | (info_ref[0] < NCTX - 1)
    return jnp.where(seen, tail, NEG)


def fill_vt(v, vt_ref):
    vt_ref[0:HD, :] = v.astype(F32).T.astype(BF)
    vt_ref[HD:, :] = jnp.ones((16, CTXL), BF)


def put_tail(t_ref, lses, dec, dec_lse):
    for m, lse in enumerate(lses):
        for n, part in enumerate(parts_of(lse)):
            t_ref[(3 * m + n) * LR : (3 * m + n + 1) * LR, :] = part
    t_ref[DECR:DSTAT, :] = dec
    for n, part in enumerate(parts_of(dec_lse)):
        t_ref[DSTAT + n : DSTAT + n + 1, :] = part
    t_ref[DSTAT + 3 :, :] = jnp.zeros((TAIL - DSTAT - 3, HD), F32)


def get_tail(t):
    t = t.astype(F32)
    lses = [sum(t[(3 * m + n) * LR : (3 * m + n + 1) * LR] for n in range(3)) for m in range(2)]
    dec_lse = t[DSTAT : DSTAT + 1] + t[DSTAT + 1 : DSTAT + 2] + t[DSTAT + 2 : DSTAT + 3]
    return lses, t[DECR:DSTAT], dec_lse


def flash_kernel(other, info_ref, q_ref, k_ref, v_ref, after_ref, x_ref, lse_ref, vt_ref, s_ref):
    i = pl.program_id(0)

    @pl.when(i == 0)
    def _():
        fill_vt(v_ref[0], vt_ref)

    s_ref[...] = scores_t(k_ref[0], q_ref[...])
    s_ref[CTXL - SLAB :, :] = masked_tail(info_ref, info_ref[1] ^ other, i, s_ref[CTXL - SLAB :, :])
    top = jnp.max(s_ref[...], axis=0, keepdims=True)
    p = jnp.exp2((s_ref[...] - top) * C2).astype(BF)
    acc = jnp.dot(vt_ref[...], p, preferred_element_type=F32)
    mass = acc[HD : HD + 1]
    x_ref[...] = (acc[0:HD] * (1.0 / mass)).T.astype(BF)
    lse = top * C2 + jnp.log2(mass)
    for j in range(RB // HD):
        lse_ref[pl.ds(i * (RB // HD) + j, 1), :] = lse[:, j * HD : (j + 1) * HD]


def flash(other, info, q, kv, after):
    return pl.pallas_call(
        functools.partial(flash_kernel, other),
        out_shape=(jax.ShapeDtypeStruct((HALF, HD), BF), jax.ShapeDtypeStruct((LR, HD), F32)),
        grid=(NRB,),
        in_specs=[
            pl.BlockSpec(memory_space=pltpu.SMEM),
            pl.BlockSpec((RB, HD), lambda i: (i, 0)),
            pl.BlockSpec((1, CTXL, HD), lambda i: (0, 0, 0)),
            pl.BlockSpec((1, CTXL, HD), lambda i: (1, 0, 0)),
            pl.BlockSpec((8, HD), lambda i: (0, 0)),
        ],
        out_specs=(pl.BlockSpec((RB, HD), lambda i: (i, 0)), pl.BlockSpec((LR, HD), lambda i: (0, 0))),
        scratch_shapes=[pltpu.VMEM((HD + 16, CTXL), BF), pltpu.VMEM((CTXL, RB), F32)],
        compiler_params=params(),
        cost_estimate=pl.CostEstimate(
            flops=20000000000, bytes_accessed=2 * CTXL * HD * 2, transcendentals=HALF * CTXL
        ),
        name="slab_partial",
    )(info, q, kv, kv, after)


def decode_kernel(flag_ref, q_ref, k_ref, v_ref, d_ref, vt_ref, s_ref):
    fill_vt(v_ref[0], vt_ref)
    for b in range(CTXL // BLK):
        s = scores_t(k_ref[0, b * BLK : (b + 1) * BLK, :], q_ref[...])
        kept = jnp.broadcast_to(flag_ref[b], s.shape) > 0
        s_ref[b * BLK : (b + 1) * BLK, :] = jnp.where(kept, s, NEG)
    top = jnp.max(s_ref[...], axis=0, keepdims=True)
    p = jnp.exp2((s_ref[...] - top) * C2).astype(BF)
    acc = jnp.dot(vt_ref[...], p, preferred_element_type=F32)
    mass = acc[HD : HD + 1]
    out = (acc[0:HD] * (1.0 / mass)).T
    lse = jnp.maximum(top * C2 + jnp.log2(mass), NEG)
    d_ref[...] = jnp.zeros_like(d_ref)
    d_ref[0:STEPR, :] = out[0:STEPR]
    d_ref[STEPR : STEPR + 1, :] = lse


def decode_partial(flags, q, kv):
    return pl.pallas_call(
        decode_kernel,
        out_shape=jax.ShapeDtypeStruct((DEC, HD), F32),
        grid=(1,),
        in_specs=[
            pl.BlockSpec(memory_space=pltpu.SMEM),
            pl.BlockSpec((HD, HD), lambda i: (0, 0)),
            pl.BlockSpec((1, CTXL, HD), lambda i: (0, 0, 0)),
            pl.BlockSpec((1, CTXL, HD), lambda i: (1, 0, 0)),
        ],
        out_specs=pl.BlockSpec((DEC, HD), lambda i: (0, 0)),
        scratch_shapes=[
            pltpu.VMEM((HD + 16, CTXL), BF),
            pltpu.VMEM((CTXL, HD), F32),
        ],
        compiler_params=params(),
        name="decode_partial",
    )(flags, q, kv, kv)


def merge_weights(lses):
    top = lses[0]
    for x in lses[1:]:
        top = jnp.maximum(top, x)
    es = [jnp.exp2(x - top) for x in lses]
    den = es[0]
    for e in es[1:]:
        den = den + e
    inv = 1.0 / den
    return [e * inv for e in es], top + jnp.log2(den)


def merge_tails(tails, t_ref):
    shares, lse = merge_weights([t[0][0] for t in tails])
    _, lse_other = merge_weights([t[0][1] for t in tails])
    dec_shares, dec_lse = merge_weights([t[2] for t in tails])
    dec = sum(t[1] * column(u)[0:STEPR] for t, u in zip(tails, dec_shares))
    put_tail(t_ref, (lse, lse_other), dec, dec_lse)
    return shares, (lse, lse_other), dec, dec_lse


def put_shares(w_ref, shares):
    for n, share in enumerate(shares):
        w_ref[0:LR, n, :] = share
        w_ref[LR, n, :] = jnp.zeros((HD,), F32)


def mix(pieces, w_ref, owner):
    first = owner * ROWS
    both = jnp.concatenate([w_ref[first // HD], w_ref[first // HD + 1]], axis=1)
    own = pltpu.roll(both, (2 * HD - first % HD) % (2 * HD), 1)[:, 0:HD]
    return sum(piece.astype(F32) * column(own[n : n + 1])[0:ROWS] for n, piece in enumerate(pieces))


def pair_kernel(info_ref, a_ref, b_ref, lo_ref, la_ref, da_ref, sb_ref, m_ref, t_ref):
    mine = ((la_ref[...], lo_ref[...]), da_ref[0:STEPR, :], da_ref[STEPR : STEPR + 1, :])
    small = sb_ref[...]
    lse_b, lse_p = small[0:LR], small[16 : 16 + LR]
    theirs = ((lse_b, lse_p), small[32 : 32 + STEPR], small[32 + STEPR : 33 + STEPR])
    (wa, wb), _, _, _ = merge_tails([mine, theirs], t_ref)
    tail = t_ref[...].astype(BF)
    for s in range(NQ):
        m_ref[s, QROWS:, :] = tail
    zl = info_ref[2] % NQ
    for g in range(LR):
        rows = slice(g * HD, (g + 1) * HD)
        a, b = a_ref[rows, :].astype(F32), b_ref[rows, :].astype(F32)
        mixed = (a * column(wa[g : g + 1]) + b * column(wb[g : g + 1])).astype(BF)
        for j in range(0, HD, 32):
            n, at = divmod(g * HD + j, ROWS)
            at += n // NQ * ROWS
            m_ref[zl ^ (n % NQ), at : at + 32, :] = mixed[j : j + 32]


def pair_merge(info, *parts):
    return pl.pallas_call(
        pair_kernel,
        out_shape=jax.ShapeDtypeStruct((NQ, QROWS + TAIL, HD), BF),
        in_specs=[pl.BlockSpec(memory_space=pltpu.SMEM)] + [pl.BlockSpec(memory_space=pltpu.VMEM)] * 6,
        out_specs=pl.BlockSpec(memory_space=pltpu.VMEM),
        scratch_shapes=[pltpu.VMEM((TAIL, HD), F32)],
        compiler_params=params(),
        name="pair_merge",
    )(info, *parts)


def quad_kernel(info_ref, a_ref, b_ref, c_ref, d_ref, z_ref, t_ref, w_ref):
    refs = (a_ref, b_ref, c_ref, d_ref)
    shares, _, _, _ = merge_tails([get_tail(ref[QROWS:, :]) for ref in refs], t_ref)
    put_shares(w_ref, shares)
    tail = t_ref[...].astype(BF)
    zl, zh = info_ref[2] % NQ, info_ref[2] // NQ
    for k in range(NZ // NQ):
        rows = slice(k * ROWS, (k + 1) * ROWS)
        z_ref[zh ^ k, 0:ROWS, :] = mix([ref[rows, :] for ref in refs], w_ref, NQ * k + zl).astype(BF)
        z_ref[k, ROWS:, :] = tail


def quad_merge(info, parts):
    return pl.pallas_call(
        quad_kernel,
        out_shape=jax.ShapeDtypeStruct((NZ // NQ, ROWS + TAIL, HD), BF),
        in_specs=[pl.BlockSpec(memory_space=pltpu.SMEM)] + [pl.BlockSpec(memory_space=pltpu.VMEM)] * 4,
        out_specs=pl.BlockSpec(memory_space=pltpu.VMEM),
        scratch_shapes=[pltpu.VMEM((TAIL, HD), F32), pltpu.VMEM((LR + 1, 8, HD), F32)],
        compiler_params=params(),
        cost_estimate=pl.CostEstimate(flops=100000000000, bytes_accessed=1 << 20, transcendentals=0),
        name="quad_merge",
    )(info, *parts)


def final_kernel(info_ref, a_ref, b_ref, c_ref, d_ref, q_ref, nk_ref, nv_ref, after_ref, slab_ref, lse_ref, step_ref, t_ref, w_ref):
    refs = (a_ref, b_ref, c_ref, d_ref)
    tails = [get_tail(ref[ROWS:, :]) for ref in refs]
    shares, lses, dec, dec_lse = merge_tails(tails, t_ref)
    lse_ref[0:LR, :] = lses[0]
    lse_ref[LR:, :] = lses[1]
    put_shares(w_ref, shares)
    slab_ref[...] = mix([ref[0:ROWS, :] for ref in refs], w_ref, info_ref[2]).astype(BF)
    fresh = scores_t(nk_ref[...], q_ref[...]) * C2
    lane = lax.broadcasted_iota(jnp.int32, (1, HD), 1)
    second = jnp.where(lane % 2 == 1, fresh[1:2], NEG)
    (kept, new_0, new_1), _ = merge_weights([dec_lse, fresh[0:1], second])
    nv = nv_ref[...].astype(F32)
    out = dec * column(kept)[0:STEPR]
    out = out + column(new_0)[0:STEPR] * nv[0:1] + column(new_1)[0:STEPR] * nv[1:2]
    step_ref[...] = out.astype(BF)


def final_merge(info, parts, q, nk, nv, after):
    return pl.pallas_call(
        final_kernel,
        out_shape=(
            jax.ShapeDtypeStruct((ROWS, HD), BF),
            jax.ShapeDtypeStruct((2 * LR, HD), F32),
            jax.ShapeDtypeStruct((STEPR, HD), BF),
        ),
        in_specs=[pl.BlockSpec(memory_space=pltpu.SMEM)] + [pl.BlockSpec(memory_space=pltpu.VMEM)] * 8,
        out_specs=[pl.BlockSpec(memory_space=pltpu.VMEM)] * 3,
        scratch_shapes=[pltpu.VMEM((TAIL, HD), F32), pltpu.VMEM((LR + 1, 8, HD), F32)],
        compiler_params=params(),
        name="final_merge",
    )(info, *parts, q, nk, nv, after)


def heavy_kernel(info_ref, q_ref, k_ref, lse_ref, h_ref, acc_ref):
    i = pl.program_id(0)

    @pl.when(i == 0)
    def _():
        acc_ref[...] = jnp.zeros_like(acc_ref)

    q = q_ref[...]
    per = RB // HD
    other = i // NRB
    lse = jnp.concatenate([lse_ref[pl.ds(i * per + j, 1), :] for j in range(per)], axis=1)
    for c in range(CTXL // SLAB):
        keys = slice(c * SLAB, (c + 1) * SLAB)
        s = scores_t(k_ref[0, keys, :], q)
        if c == CTXL // SLAB - 1:
            s = masked_tail(info_ref, info_ref[1] ^ other, i - other * NRB, s)
        w = jnp.exp2(s * C2 - lse)
        acc_ref[keys, :] += (w[:, 0:128] + w[:, 128:256]) + (w[:, 256:384] + w[:, 384:512])

    @pl.when(i == 2 * NRB - 1)
    def _():
        for t in range(CTXL // HD):
            at = slice(t * HD, (t + 1) * HD)
            sums = jnp.sum(acc_ref[at, :].T, axis=0, keepdims=True)
            h_ref[:, at] = sums * (NCTX * CTXL / (12 * SLAB))


def heavy(info, q, kv, lse):
    return pl.pallas_call(
        heavy_kernel,
        out_shape=jax.ShapeDtypeStruct((1, CTXL), F32),
        grid=(2 * NRB,),
        in_specs=[
            pl.BlockSpec(memory_space=pltpu.SMEM),
            pl.BlockSpec((RB, HD), lambda i: (i, 0)),
            pl.BlockSpec((1, CTXL, HD), lambda i: (0, 0, 0)),
            pl.BlockSpec((2 * LR, HD), lambda i: (0, 0)),
        ],
        out_specs=pl.BlockSpec((1, CTXL), lambda i: (0, 0)),
        scratch_shapes=[pltpu.VMEM((CTXL, HD), F32)],
        compiler_params=params(60),
        cost_estimate=pl.CostEstimate(
            flops=4 * HALF * CTXL * HD, bytes_accessed=CTXL * HD * 2, transcendentals=2 * HALF * CTXL
        ),
        name="heavy_columns",
    )(info, q, kv, lse)


def pack_kernel(spans, pick_ref, kv_ref, after_ref, out_ref, sems):
    copies, at = [], 0
    for n, (part, start, count) in enumerate(spans):
        for d in range(NCTX):
            source = kv_ref.at[part, pick_ref[d], start : start + count]
            copies.append(pltpu.make_async_copy(source, out_ref.at[d, at : at + count], sems.at[n, d]))
        at += count
    for copy in copies:
        copy.start()
    for copy in copies:
        copy.wait()


def pack(spans, pick, blocks, after):
    return pl.pallas_call(
        functools.partial(pack_kernel, spans),
        out_shape=jax.ShapeDtypeStruct((NCTX, sum(span[2] for span in spans), HD), BF),
        in_specs=[pl.BlockSpec(memory_space=pltpu.SMEM)] + [pl.BlockSpec(memory_space=pltpu.VMEM)] * 2,
        out_specs=pl.BlockSpec(memory_space=pl.ANY),
        scratch_shapes=[pltpu.SemaphoreType.DMA((len(spans), NCTX))],
        compiler_params=params(),
        name="pack_blocks",
    )(pick, blocks, after)


def held_kernel(x_ref, after_ref, out_ref):
    out_ref[...] = x_ref[...]


def held(x, other):
    return pl.pallas_call(
        held_kernel,
        out_shape=jax.ShapeDtypeStruct(x.shape, x.dtype),
        compiler_params=params(),
        name="held",
    )(x, other)


def picked_kernel(x_ref, out_ref):
    out_ref[...] = x_ref[...]


def picked(x):
    return pl.pallas_call(
        picked_kernel,
        out_shape=jax.ShapeDtypeStruct(x.shape, x.dtype),
        compiler_params=params(),
        cost_estimate=pl.CostEstimate(flops=1000000000, bytes_accessed=4096, transcendentals=0),
        name="picked",
    )(x)


def after_kernel(x_ref, after_ref, out_ref):
    del x_ref, after_ref, out_ref


def after(x, other):
    return pl.pallas_call(
        after_kernel,
        out_shape=jax.ShapeDtypeStruct(x.shape, x.dtype),
        in_specs=[pl.BlockSpec(memory_space=pl.ANY), pl.BlockSpec(memory_space=pltpu.VMEM)],
        out_specs=pl.BlockSpec(memory_space=pl.ANY),
        input_output_aliases={0: 0},
        name="after",
    )(x, other)


def select_kernel(src_ref, a_ref, b_ref, out_ref, sems):
    copies = []
    for r in range(SLOTS):
        at = src_ref[r]
        for n, (source, target) in enumerate((
            (a_ref.at[at, 0:BLK], out_ref.at[0, r]),
            (a_ref.at[at, BLK : BLK + FIRST], out_ref.at[1, r, 0:FIRST]),
            (b_ref.at[at], out_ref.at[1, r, FIRST:BLK]),
        )):
            copies.append(pltpu.make_async_copy(source, target, sems.at[n, r]))
    for copy in copies:
        copy.start()
    for copy in copies:
        copy.wait()


def select(source, first, second):
    return pl.pallas_call(
        select_kernel,
        out_shape=jax.ShapeDtypeStruct((2, SLOTS, BLK, HD), BF),
        in_specs=[pl.BlockSpec(memory_space=pltpu.SMEM)] + [pl.BlockSpec(memory_space=pl.ANY)] * 2,
        out_specs=pl.BlockSpec(memory_space=pltpu.VMEM),
        scratch_shapes=[pltpu.SemaphoreType.DMA((3, SLOTS))],
        compiler_params=params(),
        name="select_slots",
    )(source, first, second)


def spread_kernel(q_ref, out_ref):
    for n in range(NZ // 2):
        out_ref[n] = q_ref[...]


def spread(q):
    return pl.pallas_call(
        spread_kernel,
        out_shape=jax.ShapeDtypeStruct((NZ // 2, ROWS, HD), BF),
        compiler_params=params(),
        name="spread_queries",
    )(q)


SWAP = [(0, 1), (1, 0)]


CTX = ("xl", "zh", "zm", "zp")
BLOCKS = ("zh", "zm", "zp", "xl")


def local(slab_query, kv_cache, kept_list, decode_place, step_query, step_cache):
    grp = lax.axis_index("grp")
    xl = lax.axis_index("xl")
    zp = lax.axis_index("zp")
    z = lax.axis_index("zh") * NQ + lax.axis_index("zm") * 2 + zp
    ctx = xl * NZ + z
    per_dev = CTXL // BLK

    kept = lax.dynamic_index_in_dim(kept_list, 1 - grp, 0, keepdims=False)[0]
    place = lax.dynamic_index_in_dim(decode_place, 1 - grp, 0, keepdims=False)[0]
    slots = jnp.arange(NCTX, dtype=jnp.int32)
    lanes = slots % 2 * NZ + slots // 2
    offset = kept - ctx * per_dev
    mine = (offset >= 0) & (offset < per_dev)
    hit = mine[None, :] & (place[None, :] == lanes[:, None])
    pick = jnp.clip(jnp.sum(jnp.where(hit, offset[None, :], 0), axis=1), 0, per_dev - 1)
    flags = jnp.sum(
        (offset[None, :] == jnp.arange(per_dev, dtype=jnp.int32)[:, None]).astype(jnp.int32), axis=1
    )
    here = (place == ctx).reshape(SLOTS, NCTX)
    owner = jnp.sum(jnp.where(here, kept.reshape(SLOTS, NCTX) // per_dev, 0), axis=1)
    source = jnp.clip(owner % NZ * 2 + owner // NZ, 0, NCTX - 1)
    info = jnp.stack([ctx, xl, z]).astype(jnp.int32)

    q = jnp.transpose(slab_query[0, :, 0], (1, 0, 2)).reshape(ROWS, HD)
    kv = kv_cache[0, :, :, 0]
    steps = jnp.transpose(step_query[0, :, 0], (1, 0, 2)).reshape(STEPR, HD)
    steps = jnp.pad(steps, ((0, HD - STEPR), (0, 0)))
    new = jnp.pad(step_cache[0, :, :, 0], ((0, 0), (0, 14), (0, 0)))

    kv_decode = lax.ppermute(kv, "grp", SWAP)
    blocks = kv_decode.reshape(2, per_dev, BLK, HD)
    q_same = lax.all_to_all(spread(q), ("zh", "zm"), 0, 0, tiled=True)
    pick = picked(pick.reshape(1, NCTX)).reshape(NCTX)
    packed = pack(((0, 0, BLK), (1, 0, FIRST)), pick, blocks, steps[0:16])
    q_next = lax.ppermute(held(q_same, packed[0, 0:16]), "zp", SWAP)
    even, odd = jnp.where(zp == 0, q_same, q_next), jnp.where(zp == 0, q_next, q_same)
    q_own = jnp.stack([even, odd], axis=1).reshape(HALF, HD)
    dec = decode_partial(flags, steps, kv_decode)

    keys = lax.all_to_all(packed, BLOCKS, 0, 0, tiled=True)
    q_other = lax.ppermute(q_own, "xl", SWAP)
    part_own, lse_own = flash(0, info, q_own, kv, dec[0:8])
    part_other, lse_other = flash(1, info, q_other, kv, lse_own[0:8])
    blank = jnp.zeros((16 - LR, HD), F32)
    small = lax.ppermute(jnp.concatenate([lse_other, blank, lse_own, blank, dec], axis=0), "xl", SWAP)
    part_beside = lax.ppermute(part_other, "xl", SWAP)
    parts = pair_merge(info, part_own, part_beside, lse_other, lse_own, dec, small)
    near = [lax.ppermute(parts[s], ("zm", "zp"), [(i, i ^ s) for i in range(NQ)]) for s in range(1, NQ)]
    rest = pack(((1, FIRST, BLK - FIRST),), pick, blocks, parts[0, 0:16])
    values = lax.all_to_all(after(rest, keys[0, 0:16]), BLOCKS, 0, 0, tiled=True)
    merged = quad_merge(info, [parts[0]] + near)
    far = [lax.ppermute(merged[s], "zh", [(i, i ^ s) for i in range(NZ // NQ)]) for s in range(1, NZ // NQ)]
    paged = select(source, keys, values)
    slab, lse, step = final_merge(info, [merged[0]] + far, steps, new[0], new[1], paged[0, 0, 0:16])
    columns = heavy(info, jnp.concatenate([q_own, q_other], axis=0), kv, lse)

    slab_out = jnp.transpose(slab.reshape(12, 8, HD), (1, 0, 2))[None, :, None]
    step_out = jnp.transpose(step.reshape(12, 2, HD), (1, 0, 2))[None, :, None]
    return (slab_out, columns[None], paged[None, None], step_out)


def solution(mesh):
    split = Mesh(mesh.devices.reshape(2, 2, NZ // NQ, 2, 2, 8), ("grp", "xl", "zh", "zm", "zp", "kvh"))
    return jax.shard_map(
        local,
        mesh=split,
        in_specs=(
            P("grp", CTX, "kvh", None, None),
            P("grp", None, CTX, "kvh", None),
            P(None, "kvh", None),
            P(None, "kvh", None),
            P("grp", None, "kvh", None, None),
            P("grp", None, None, "kvh", None),
        ),
        out_specs=(
            P("grp", CTX, "kvh", None, None),
            P("grp", "kvh", CTX),
            P("grp", "kvh", None, CTX, None, None),
            P("grp", None, "kvh", None, None),
        ),
        check_vma=False,
    )
```
